128 devices in a mesh: hi: 8 (over x_hi, z), lo: 16 (over y, x_lo, core).
Axes of the slice: x: 4 (x_hi: 2, x_lo: 2; x = x_hi * 2 + x_lo), y: 4, z: 4, core: 2. Of those that a mesh axis runs over, the one named last changes fastest.
Arguments:
- amplitudes: float32 [8, 16, 131072], P('hi', 'lo'), may hold values from -6 to 6
- gate_stack: float32 [8, 128, 128], replicated, may hold values from -6 to 6
- targets: int32 [8, 7], replicated, may hold values from 0 to 9, as said below
Outputs:
- evolved: float32 [8, 16, 131072], P('hi', 'lo')
The draws below stay inside these ranges and needn't reach their ends.
Inputs may be any that keep to these rules, and one draw needn't show every extreme that they name: `targets`: the seven entries of each row are distinct; the first row holds 0 and 9.
All inputs are finite; a program needn't handle non-finite values.
Results may differ from the reference program's by a relative error of at most 0.00019.
Values sent between devices are 32-bit elements; how exact they have to be, the bound alone decides.
No kernel may reach another device: no remote copies, remote signals or barrier semaphores. Data moves between devices by JAX's collectives and lax.ppermute only.
A program may use at most 64 MiB of HBM per device.

```python
import jax
import jax.numpy as jnp
from jax import lax

AMPS = 131072
LAYERS = 8
SPAN = 10
GATE = 128
N_HI = 8
N_LO = 16


def draw_targets(key, part):
    key = jax.random.fold_in(key, 11)
    row_keys = jax.random.split(key, LAYERS)
    layer_rows = jax.vmap(lambda row_key: jax.random.permutation(row_key, SPAN)[:7])(row_keys)
    middle = jax.random.permutation(jax.random.fold_in(key, 5), SPAN - 2)[:5] + 1
    first_row = jnp.concatenate([jnp.array([0, SPAN - 1], dtype=jnp.int32), middle.astype(jnp.int32)])
    first_row = jax.random.permutation(jax.random.fold_in(key, 7), first_row)
    return layer_rows.astype(jnp.int32).at[0].set(first_row)


def steps_of(key, dims, cuts, low, largest):
    factor_of = 1.0
    for dim, parts in cuts:
        draws = jax.random.uniform(jax.random.fold_in(jax.random.fold_in(key, 6), dim), (parts,), jnp.float32, low / len(cuts), largest / len(cuts))
        factor_of = factor_of * jnp.repeat(jnp.exp(draws), dims[dim] // parts).reshape((-1,) + (1,) * (len(dims) - 1 - dim))
    return factor_of


def centred(key, extent, width, limit, cuts=(), kind=jnp.bfloat16):
    level = steps_of(key, extent, cuts, -0.22, 0.18) if cuts else 1.0
    drawn = jax.random.normal(key, extent, jnp.float32) * width * level
    return jnp.minimum(jnp.maximum(drawn, -limit), limit).astype(kind)


def setup_inputs(seed: int = 0) -> dict:
    key_list = jax.random.split(jax.random.key(seed), 4)
    return {
        "amplitudes": centred(key_list[0], (N_HI, N_LO, AMPS), 1.0, 6.0, ((0, 8), (1, 16)), jnp.float32),
        "gate_stack": centred(key_list[1], (LAYERS, GATE, GATE), 1.0, 6.0, (), jnp.float32),
        "targets": draw_targets(jax.random.fold_in(key_list[3], 71), 0),
    }


def build_gates(gate_stack):
    layer_count = gate_stack.shape[0]
    order = gate_stack.shape[1]
    start = jnp.broadcast_to(jnp.eye(order, dtype=jnp.float32), (layer_count, order, order))

    def reflect(current, vectors):
        lengths = jnp.sum(vectors * vectors, axis=1)
        images = jnp.einsum("lij,lj->li", current, vectors, precision=lax.Precision.HIGHEST)
        scaled = images * (2.0 / lengths)[:, None]
        return current - scaled[:, :, None] * vectors[:, None, :], None

    result, unused = lax.scan(reflect, start, jnp.transpose(gate_stack, (1, 0, 2)))
    return result


def bit_moves(chosen, index_bits, picked):
    position_ids = jnp.arange(2 ** index_bits, dtype=jnp.int32)
    slot_ids = jnp.arange(picked, dtype=jnp.int32)
    source_index = jnp.zeros_like(position_ids)
    place_index = jnp.zeros_like(position_ids)
    for position in range(index_bits):
        matches = chosen == position
        slot_of = jnp.sum(jnp.where(matches, slot_ids, 0)).astype(jnp.int32)
        lower_count = jnp.sum((chosen < position).astype(jnp.int32))
        new_place = jnp.where(jnp.any(matches), slot_of, picked + position - lower_count).astype(jnp.int32)
        source_index = source_index | (((position_ids >> new_place) & 1) << position)
        place_index = place_index | (((position_ids >> position) & 1) << new_place)
    return source_index, place_index


def apply_rows(blocks, gate_matrix):
    return jnp.dot(blocks, gate_matrix.T, precision=lax.Precision.HIGHEST, preferred_element_type=jnp.float32)


def reference(amplitudes, gate_stack, targets):
    total_bits = AMPS.bit_length() - 1
    lo_bits = N_LO.bit_length() - 1
    hi_bits = N_HI.bit_length() - 1
    gate_matrices = build_gates(gate_stack)
    current = amplitudes
    for layer_index in range(LAYERS):
        gate_matrix = gate_matrices[layer_index]
        chosen = targets[layer_index]
        layer_kind = layer_index % 4
        if layer_kind == 0 or layer_kind == 2:
            source_index, place_index = bit_moves(chosen, total_bits, 7)
            permuted = jnp.take(current, source_index, axis=2).reshape(-1, 128)
            permuted = apply_rows(permuted, gate_matrix).reshape(N_HI, N_LO, AMPS)
            current = jnp.take(permuted, place_index, axis=2)
        elif layer_kind == 1:
            hi_bit = (layer_index // 4) % hi_bits
            upper_count = N_HI >> (hi_bit + 1)
            lower_count = 2 ** hi_bit
            source_index, place_index = bit_moves(chosen[:6], total_bits, 6)
            permuted = jnp.take(current, source_index, axis=2)
            blocks = permuted.reshape(upper_count, 2, lower_count, N_LO, AMPS // 64, 64)
            blocks = blocks.transpose(0, 2, 3, 4, 1, 5).reshape(-1, 128)
            blocks = apply_rows(blocks, gate_matrix)
            blocks = blocks.reshape(upper_count, lower_count, N_LO, AMPS // 64, 2, 64)
            blocks = blocks.transpose(0, 4, 1, 2, 3, 5).reshape(N_HI, N_LO, AMPS)
            current = jnp.take(blocks, place_index, axis=2)
        else:
            group_width = 128 // N_LO
            picked = 7 - lo_bits
            source_index, place_index = bit_moves(chosen[:picked], total_bits, picked)
            permuted = jnp.take(current, source_index, axis=2)
            blocks = permuted.reshape(N_HI, N_LO, AMPS // group_width, group_width)
            blocks = blocks.transpose(0, 2, 1, 3).reshape(-1, 128)
            blocks = apply_rows(blocks, gate_matrix)
            blocks = blocks.reshape(N_HI, AMPS // group_width, N_LO, group_width)
            blocks = blocks.transpose(0, 2, 1, 3).reshape(N_HI, N_LO, AMPS)
            current = jnp.take(blocks, place_index, axis=2)
    return current
```

```python
import jax
import jax.numpy as jnp
from jax import lax
from jax.experimental import pallas as pl
from jax.experimental.pallas import tpu as pltpu
from jax.sharding import Mesh
from jax.sharding import PartitionSpec as P

LAYERS = 8
SPAN = 10
WIDE = 1 << SPAN
GATE = 128
F32 = jnp.float32
BF16 = jnp.bfloat16
ROWS = 128
PICKED = (7, 6, 7, 3)


def two_parts(value):
    high = value.astype(BF16)
    return high, (value - high.astype(F32)).astype(BF16)


def three_parts(value):
    high = value.astype(BF16)
    left = value - high.astype(F32)
    middle = left.astype(BF16)
    return high, middle, (left - middle.astype(F32)).astype(BF16)


def dot(left, right):
    return lax.dot_general(left, right, (((1,), (0,)), ((), ())), preferred_element_type=F32)


def left_form(value):
    high, middle, low = three_parts(value)
    return jnp.concatenate([high, middle], 1), jnp.concatenate([high, low], 1)


def right_form(value):
    high, middle, low = three_parts(value)
    both = jnp.concatenate([high, middle], 1)
    return jnp.concatenate([both, both], 0), jnp.concatenate([low, high], 0)


def full_dot(left, right):
    first = dot(left[0], right[0])
    return first[:, :GATE] + (first[:, GATE:] + dot(left[1], right[1]))


def bit_places(targets_ref, layer):
    kind = layer % 4
    picked = PICKED[kind]
    chosen = [targets_ref[layer, j] for j in range(picked)]
    rest = []
    count = SPAN - picked
    taken = [sum((chosen[j] == q).astype(jnp.int32) for j in range(picked)) for q in range(SPAN)]
    rank = []
    free = jnp.int32(0)
    for q in range(SPAN):
        rank.append(free)
        free = free + 1 - taken[q]
    for k in range(count):
        place = jnp.int32(0)
        for q in range(SPAN):
            place = place + jnp.where((rank[q] == k) & (taken[q] == 0), q, 0)
        rest.append(place)
    return rest + chosen if kind == 3 else chosen + rest


def natural(position, places, low, high):
    value = jnp.zeros_like(position)
    for m in range(low, high):
        value = value + (((position >> m) & 1) << places[m])
    return value


def prepare_kernel(targets_ref, stack_ref, moves_ref, gates_ref, moved, state, low_tri, sems):
    identity = list(range(SPAN))
    places = [identity] + [bit_places(targets_ref, layer) for layer in range(LAYERS)] + [identity]
    lanes = lax.broadcasted_iota(jnp.int32, (16, WIDE), 1)
    subs = lax.broadcasted_iota(jnp.int32, (16, WIDE), 0)
    copies = []
    for k in range(LAYERS + 1):
        slot = k % 2
        if k >= 2:
            copies[k - 2].wait()
        source, target = places[k], places[k + 1]
        wanted = natural(lanes, target, 0, SPAN) - natural(subs, source, 0, 4)

        def rows(block, carry, source=source, wanted=wanted, slot=slot):
            base = natural(block * 16, source, 4, SPAN)
            moved[slot, pl.ds(pl.multiple_of(block * 16, 16), 16), :] = jnp.where(wanted == base, 1.0, 0.0).astype(BF16)
            return carry

        lax.fori_loop(0, WIDE // 16, rows, 0)
        copy = pltpu.make_async_copy(moved.at[slot], moves_ref.at[k], sems.at[slot])
        copy.start()
        copies.append(copy)
    row = lax.broadcasted_iota(jnp.int32, (GATE, GATE), 0)
    col = lax.broadcasted_iota(jnp.int32, (GATE, GATE), 1)
    shuffle = (row == ((col & 15) << 3 | col >> 4)).astype(F32)
    shuffle_right = right_form(shuffle)
    units, units_t = [], []
    for g in range(LAYERS):
        vectors = stack_ref[g]
        lengths = jnp.sum(vectors * vectors, axis=1, keepdims=True)
        unit = vectors * lax.rsqrt(lengths)
        if g % 4 == 3:
            unit = full_dot(left_form(unit), shuffle_right)
        units.append(unit)
        units_t.append(unit.T)
    for g in range(LAYERS):
        gram = full_dot(left_form(units[g]), right_form(units_t[g]))
        low_tri[g] = gram
        state[g] = jnp.where(row == col, 2.0 / gram, 0.0)

    def level(step, carry):
        bit = jnp.int32(1) << step
        same = (row >> (step + 1)) == (col >> (step + 1))
        row_set = (row & bit) != 0
        col_set = (col & bit) != 0
        lower = same & row_set & ~col_set
        upper = same & col_set & ~row_set
        for g in range(LAYERS):
            cut = jnp.where(upper if g % 4 == 3 else lower, low_tri[g], 0.0)
            now = state[g]
            first = full_dot(left_form(now), right_form(cut))
            state[g] = now - full_dot(left_form(first), right_form(now))
        return carry

    lax.fori_loop(0, 7, level, 0)
    lane_low = col < 64
    for g in range(LAYERS):
        inner = full_dot(left_form(state[g]), right_form(units[g]))
        gate = jnp.where(row == col, 1.0, 0.0) - full_dot(left_form(units_t[g]), right_form(inner))
        high, low = two_parts(gate)
        if g % 4 == 3:
            gates_ref[g, 0, :GATE, :] = jnp.concatenate([high, high], 1)
            gates_ref[g, 0, GATE:, :] = jnp.concatenate([low, low], 1)
        elif g % 4 == 1:
            turned = pltpu.roll(gate, 64, 1)
            for b in range(2):
                own = gate[64 * b : 64 * b + 64]
                other = turned[64 * b : 64 * b + 64]
                left = lane_low[:64]
                for a in range(2):
                    twice = jnp.where(left, own, other) if a == 0 else jnp.where(left, other, own)
                    block = jnp.concatenate([jnp.where(left, twice, 0.0), jnp.where(left, 0.0, twice)], 0)
                    parts = two_parts(block)
                    for part in range(2):
                        gates_ref[g, part, GATE * b : GATE * (b + 1), GATE * a : GATE * (a + 1)] = parts[part]
        else:
            both = jnp.concatenate([high, low], 1)
            gates_ref[g, 0, :GATE, :] = both
            gates_ref[g, 0, GATE:, :] = both
    copies[-2].wait()
    copies[-1].wait()


def prepare(targets, gate_stack):
    return pl.pallas_call(
        prepare_kernel,
        out_shape=(
            jax.ShapeDtypeStruct((LAYERS + 1, WIDE, WIDE), BF16),
            jax.ShapeDtypeStruct((LAYERS, 2, 2 * GATE, 2 * GATE), BF16),
        ),
        in_specs=[pl.BlockSpec(memory_space=pltpu.SMEM), pl.BlockSpec(memory_space=pltpu.VMEM)],
        out_specs=(pl.BlockSpec(memory_space=pl.ANY), pl.BlockSpec(memory_space=pltpu.VMEM)),
        scratch_shapes=[
            pltpu.VMEM((2, WIDE, WIDE), BF16),
            pltpu.VMEM((LAYERS, GATE, GATE), F32),
            pltpu.VMEM((LAYERS, GATE, GATE), F32),
            pltpu.SemaphoreType.DMA((2,)),
        ],
        compiler_params=pltpu.CompilerParams(vmem_limit_bytes=24 * 2**20),
        cost_estimate=pl.CostEstimate(flops=8 * 10**9, bytes_accessed=20 * 2**20, transcendentals=0),
        name="prepare",
    )(targets, gate_stack)


def evolve_kernel(x_ref, gates_ref, moves_hbm, out_ref, moves, now, then, sems):
    def fetch(k):
        return pltpu.make_async_copy(moves_hbm.at[k], moves.at[k % 3], sems.at[k % 3])

    fetch(0).start()
    fetch(1).start()
    for s in range(2):
        for tile in range(8):
            high, low = two_parts(x_ref[:, s * 8 + tile, :])
            lanes = slice(tile * 128, tile * 128 + 128)
            now[64 * s : 64 * s + 64, lanes] = high
            now[ROWS + 64 * s : ROWS + 64 * s + 64, lanes] = low

    def lanes_of(n):
        return pl.ds(pl.multiple_of(n * 256, 256), 256)

    for k in range(LAYERS + 1):
        if k + 2 <= LAYERS:
            fetch(k + 2).start()
        fetch(k).wait()
        move = moves.at[k % 3]
        source, target = (now, then) if k % 2 == 0 else (then, now)
        kind = 4 if k == LAYERS else k % 4

        def block(n, carry, k=k, kind=kind, move=move, source=source, target=target):
            moved = dot(source[...], move[:, lanes_of(n)])
            if kind == 4:
                total = moved[:ROWS] + moved[ROWS:]
                for half in range(2):
                    for s in range(2):
                        out_ref[:, s * 8 + n * 2 + half, :] = total[64 * s : 64 * s + 64, 128 * half : 128 * half + 128]
                return carry
            moved = moved.astype(BF16)
            if kind == 3:
                target[:, lanes_of(n)] = moved
                return carry
            high, low = moved[:ROWS], moved[ROWS:]
            if kind == 1:
                width = 16 << (k // 4)
                groups = ROWS // (2 * width)
                zero = [slice(2 * width * i, 2 * width * i + width) for i in range(groups)]
                one = [slice(2 * width * i + width, 2 * width * (i + 1)) for i in range(groups)]

                def pairs(part):
                    sides = []
                    for rows in (zero, one):
                        sides.append(jnp.concatenate([part[r, 128 * half : 128 * half + 128] for half in range(2) for r in rows], 0))
                    return jnp.concatenate(sides, 1)

                high_pairs, low_pairs = pairs(high), pairs(low)
                out = dot(high_pairs, gates_ref[k, 0]) + dot(low_pairs, gates_ref[k, 0]) + dot(high_pairs, gates_ref[k, 1])
                halves = []
                for half in range(2):
                    pieces = []
                    for i in range(groups):
                        rows = slice(64 * half + width * i, 64 * half + width * (i + 1))
                        pieces += [out[rows, :128], out[rows, 128:]]
                    halves.append(jnp.concatenate(pieces, 0))
                result = jnp.concatenate(halves, 1)
            else:
                tall = jnp.concatenate(
                    [jnp.concatenate([high[:, 128 * h : 128 * h + 128], low[:, 128 * h : 128 * h + 128]], 1) for h in range(2)], 0
                )
                out = dot(tall, gates_ref[k, 0])
                out = out[:, :128] + out[:, 128:]
                result = jnp.concatenate([out[:ROWS], out[ROWS:]], 1)
            high, low = two_parts(result)
            target[:ROWS, lanes_of(n)] = high
            target[ROWS:, lanes_of(n)] = low
            return carry

        if kind == 4:
            for n in range(4):
                block(n, 0)
        else:
            lax.fori_loop(0, 4, block, 0)
        if kind == 3:
            for q in range(0, 8, 2):
                columns = []
                for p in (q, q + 1):
                    rows = [target[part * ROWS + 16 * p : part * ROWS + 16 * p + 16, 128 * t : 128 * t + 128] for part in range(2) for t in range(8)]
                    columns.append(jnp.concatenate(rows, 0))
                out = dot(gates_ref[k, 0], jnp.concatenate(columns, 1))
                high, low = two_parts(out[:ROWS] + out[ROWS:])
                for i, p in enumerate((q, q + 1)):
                    for t in range(8):
                        rows, lanes = slice(16 * t, 16 * t + 16), slice(128 * i, 128 * i + 128)
                        target[16 * p : 16 * p + 16, 128 * t : 128 * t + 128] = high[rows, lanes]
                        target[ROWS + 16 * p : ROWS + 16 * p + 16, 128 * t : 128 * t + 128] = low[rows, lanes]


def evolve(state, gates, moves):
    return pl.pallas_call(
        evolve_kernel,
        out_shape=jax.ShapeDtypeStruct(state.shape, F32),
        in_specs=[
            pl.BlockSpec(memory_space=pltpu.VMEM),
            pl.BlockSpec(memory_space=pltpu.VMEM),
            pl.BlockSpec(memory_space=pl.ANY),
        ],
        out_specs=pl.BlockSpec(memory_space=pltpu.VMEM),
        scratch_shapes=[
            pltpu.VMEM((3, WIDE, WIDE), BF16),
            pltpu.VMEM((2 * ROWS, WIDE), BF16),
            pltpu.VMEM((2 * ROWS, WIDE), BF16),
            pltpu.SemaphoreType.DMA((3,)),
        ],
        compiler_params=pltpu.CompilerParams(vmem_limit_bytes=24 * 2**20),
        cost_estimate=pl.CostEstimate(flops=6 * 10**9, bytes_accessed=20 * 2**20, transcendentals=0),
        name="evolve",
    )(state, gates, moves)


def body(amplitudes, gate_stack, targets):
    group = ("z", "lo")
    state = amplitudes.reshape(64, 16, 128)
    state = lax.all_to_all(state, group, split_axis=0, concat_axis=0, tiled=True)
    moves, gates = prepare(targets, gate_stack)
    state = evolve(state, gates, moves)
    state = lax.all_to_all(state, group, split_axis=0, concat_axis=0, tiled=True)
    return state.reshape(amplitudes.shape)


def solution(mesh):
    split = Mesh(mesh.devices.reshape(2, 4, 16), ("top", "z", "lo"))
    in_specs = (P(("top", "z"), "lo", None), P(), P())
    out_specs = P(("top", "z"), "lo", None)
    return jax.shard_map(body, mesh=split, in_specs=in_specs, out_specs=out_specs, check_vma=False)
```

```python
import jax
import jax.numpy as jnp
from jax import lax
from jax.experimental import pallas as pl
from jax.experimental.pallas import tpu as pltpu
from jax.sharding import Mesh
from jax.sharding import PartitionSpec as P

LAYERS = 8
SPAN = 10
WIDE = 1 << SPAN
GATE = 128
FULL = WIDE - 1
LANES = GATE - 1
F32 = jnp.float32
BF16 = jnp.bfloat16
I32 = jnp.int32
PICKED = (7, 6, 7, 3)


def two_parts(value):
    high = value.astype(BF16)
    return high, (value - high.astype(F32)).astype(BF16)


def three_parts(value):
    high = value.astype(BF16)
    left = value - high.astype(F32)
    middle = left.astype(BF16)
    return high, middle, (left - middle.astype(F32)).astype(BF16)


def dot(left, right):
    return lax.dot_general(left, right, (((1,), (0,)), ((), ())), preferred_element_type=F32)


def left_form(value):
    high, middle, low = three_parts(value)
    return jnp.concatenate([high, middle], 1), jnp.concatenate([high, low], 1)


def right_form(value):
    high, middle, low = three_parts(value)
    both = jnp.concatenate([high, middle], 1)
    return jnp.concatenate([both, both], 0), jnp.concatenate([low, high], 0)


def full_dot(left, right):
    first = dot(left[0], right[0])
    return first[:, :GATE] + (first[:, GATE:] + dot(left[1], right[1]))


def lowest(mask, count):
    bits = []
    for _ in range(count):
        low = mask & -mask
        bits.append(low)
        mask = mask ^ low
    return bits


def union(bits):
    mask = bits[0]
    for bit in bits[1:]:
        mask = mask | bit
    return mask


def layer_orders(targets_ref):
    masks, tops = [LANES], [[128, 256, 512]]
    targets = []
    for layer in range(LAYERS):
        kind = layer % 4
        picked = [jnp.int32(1) << targets_ref[layer, j] for j in range(PICKED[kind])]
        targets.append(picked)
        mask = union(picked)
        other = FULL ^ mask
        if kind == 3:
            masks.append(other)
            tops.append(picked)
        else:
            masks.append(mask)
            tops.append(lowest(other, SPAN - PICKED[kind]))
    masks.append(LANES)
    tops.append([128, 256, 512])
    shared = [lowest(masks[s] & masks[s + 1], 3) for s in range(LAYERS + 1)]

    def order(stage, low):
        return low + lowest(masks[stage] ^ union(low), SPAN - 3 - len(tops[stage])) + tops[stage]

    taken = [None] + [order(s, shared[s - 1]) for s in range(1, LAYERS + 2)]
    left = [order(s, shared[s]) for s in range(LAYERS + 1)] + [None]
    return targets, taken, left


def spread(position, bits):
    value = jnp.zeros_like(position)
    for m, bit in enumerate(bits):
        value = jnp.where((position & (1 << m)) != 0, value + bit, value)
    return value


def collect(value, bits):
    position = jnp.zeros_like(value)
    for m, bit in enumerate(bits):
        position = jnp.where((value & bit) != 0, position + (1 << m), position)
    return position


def prepare_kernel(targets_ref, stack_ref, gates_ref, moves_ref, perms_ref, state, gram_ref):
    lane = lax.broadcasted_iota(I32, (8, GATE), 1)
    targets, taken, left = layer_orders(targets_ref)
    for s in range(LAYERS + 1):
        source = collect(spread(lane, taken[s + 1][3:]), left[s][3:])
        moves_ref[s] = source * 8
    natural = [1 << m for m in range(7)]
    for i, (old, new) in enumerate(
        [(natural, left[0]), (taken[4], left[4]), (taken[8], left[8]), (taken[9], natural)]
    ):
        perms_ref[i] = collect(spread(lane, new[:7]), old[:7])
    row = lax.broadcasted_iota(I32, (GATE, GATE), 0)
    col = lax.broadcasted_iota(I32, (GATE, GATE), 1)
    ins, outs, deltas = [], [], []
    for g in range(LAYERS):
        vectors = stack_ref[g]
        lengths = jnp.sum(vectors * vectors, axis=1, keepdims=True)
        unit = vectors * lax.rsqrt(lengths)
        if g % 4 == 3:
            index_in = index_out = (lane & 15) << 3 | lane >> 4
        else:
            count = PICKED[g % 4]
            index_in, index_out = (
                collect(spread(lane, order[g + 1][:count]), targets[g]) + (lane >> count << count) for order in (taken, left)
            )
        pick_in = jnp.where(row == index_in[:1], 1.0, 0.0)
        pick_out = jnp.where(row == index_out[:1], 1.0, 0.0)
        out_rows = jnp.broadcast_to(index_out[:1], (GATE, GATE)).astype(F32).T
        deltas.append(jnp.where(out_rows == index_in[:1].astype(F32), 1.0, 0.0))
        parts = dot(jnp.concatenate(three_parts(unit), 0), jnp.concatenate([pick_in, pick_out], 1).astype(BF16))
        both = parts[:GATE] + parts[GATE : 2 * GATE] + parts[2 * GATE :]
        ins.append(both[:, :GATE])
        outs.append(both[:, GATE:].T)
        gram_ref[g] = full_dot(left_form(both[:, :GATE]), right_form(both[:, :GATE].T))
        state[g] = jnp.where(row == col, 2.0 / gram_ref[g], 0.0)

    def level(step, carry):
        bit = jnp.int32(1) << step
        upper = ((row >> (step + 1)) == (col >> (step + 1))) & ((col & bit) != 0) & ((row & bit) == 0)
        for g in range(LAYERS):
            cut = jnp.where(upper, gram_ref[g], 0.0)
            now = state[g]
            first = full_dot(left_form(now), right_form(cut))
            state[g] = now - full_dot(left_form(first), right_form(now))
        return carry

    lax.fori_loop(0, 7, level, 0)
    for g in range(LAYERS):
        inner = full_dot(left_form(state[g]), right_form(ins[g]))
        gate = deltas[g] - full_dot(left_form(outs[g]), right_form(inner))
        if g % 4 == 1:
            gate = jnp.where(row < 64, gate, pltpu.roll(gate, 64, 1))
        high, low = two_parts(gate)
        gates_ref[g, :GATE, :] = jnp.concatenate([high, high], 1)
        gates_ref[g, GATE:, :] = jnp.concatenate([low, low], 1)


def prepare(targets, gate_stack):
    return pl.pallas_call(
        prepare_kernel,
        out_shape=(
            jax.ShapeDtypeStruct((LAYERS, 2 * GATE, 2 * GATE), BF16),
            jax.ShapeDtypeStruct((LAYERS + 1, 8, GATE), I32),
            jax.ShapeDtypeStruct((4, 8, GATE), I32),
        ),
        in_specs=[pl.BlockSpec(memory_space=pltpu.SMEM), pl.BlockSpec(memory_space=pltpu.VMEM)],
        out_specs=(pl.BlockSpec(memory_space=pltpu.VMEM),) * 3,
        scratch_shapes=[
            pltpu.VMEM((LAYERS, GATE, GATE), F32),
            pltpu.VMEM((LAYERS, GATE, GATE), F32),
        ],
        compiler_params=pltpu.CompilerParams(vmem_limit_bytes=24 * 2**20),
        cost_estimate=pl.CostEstimate(flops=8 * 10**9, bytes_accessed=20 * 2**20, transcendentals=0),
        name="prepare",
    )(targets, gate_stack)


def side_by_side(blocks):
    return jnp.concatenate([jnp.concatenate(block, 0) for block in blocks], 1)


def evolve_kernel(x_ref, gates_ref, moves_ref, perms_ref, out_ref, here, there, table, sem):
    copy = pltpu.make_async_copy(moves_ref, table, sem)
    copy.start()
    lane = lax.broadcasted_iota(I32, (64, GATE), 1)

    def permuted(value, i):
        return jnp.take_along_axis(value, jnp.broadcast_to(perms_ref[i, :1, :], value.shape), axis=1)

    for tile in range(8):
        value = jnp.concatenate([x_ref[:, tile, :], x_ref[:, 8 + tile, :]], 0)
        here[tile * GATE : (tile + 1) * GATE, :] = permuted(value, 0).T
    copy.wait()

    def rows(source, stage, first, count):
        return jnp.concatenate(
            [source[pl.ds(pl.multiple_of(table[stage, 0, first + i], 8), 8), :] for i in range(count)], 0
        )

    def applied(layer, blocks):
        out = dot(gates_ref[layer], side_by_side(blocks))
        return out[:GATE] + out[GATE:]

    source, target = here, there
    for layer in range(LAYERS):
        kind = layer % 4
        if kind == 1:
            width = 16 << (layer // 4)
            one = (lane & width) != 0
            for pair in range(8):
                blocks = []
                for i in range(2):
                    own = rows(source, layer, (2 * pair + i) * 8, 8)
                    other = jnp.where(one, pltpu.roll(own, width, 1), pltpu.roll(own, GATE - width, 1))
                    own, other = two_parts(own), two_parts(other)
                    blocks.append([own[0], other[0], own[1], other[1]])
                out = applied(layer, blocks)
                for i in range(2):
                    first = (2 * pair + i) * 64
                    part = out[:, GATE * i : GATE * (i + 1)]
                    target[first : first + 64, :] = jnp.where(one, part[64:], part[:64])
        elif kind == 3:
            tiles = [two_parts(rows(source, layer, tile * 16, 16).T) for tile in range(8)]
            outs = []
            for q in range(0, 8, 2):
                blocks = [
                    [tiles[t][part][16 * p : 16 * p + 16] for part in range(2) for t in range(8)] for p in (q, q + 1)
                ]
                outs.append(applied(layer, blocks))
            for tile in range(8):
                value = jnp.concatenate(
                    [outs[q // 2][16 * tile : 16 * tile + 16, GATE * (q % 2) : GATE * (q % 2 + 1)] for q in range(8)], 0
                )
                target[tile * GATE : (tile + 1) * GATE, :] = permuted(value, 1 + layer // 4).T
        else:
            for pair in range(4):
                blocks = [two_parts(rows(source, layer, (2 * pair + i) * 16, 16)) for i in range(2)]
                out = applied(layer, blocks)
                for i in range(2):
                    first = (2 * pair + i) * GATE
                    target[first : first + GATE, :] = out[:, GATE * i : GATE * (i + 1)]
        source, target = target, source
    for tile in range(8):
        value = permuted(rows(source, LAYERS, tile * 16, 16).T, 3)
        out_ref[:, tile, :] = value[:64]
        out_ref[:, 8 + tile, :] = value[64:]


def evolve(state, gates, moves, perms):
    return pl.pallas_call(
        evolve_kernel,
        out_shape=jax.ShapeDtypeStruct(state.shape, F32),
        in_specs=[pl.BlockSpec(memory_space=pltpu.VMEM)] * 4,
        out_specs=pl.BlockSpec(memory_space=pltpu.VMEM),
        scratch_shapes=[
            pltpu.VMEM((WIDE, GATE), F32),
            pltpu.VMEM((WIDE, GATE), F32),
            pltpu.SMEM((LAYERS + 1, 8, GATE), I32),
            pltpu.SemaphoreType.DMA,
        ],
        compiler_params=pltpu.CompilerParams(vmem_limit_bytes=24 * 2**20),
        cost_estimate=pl.CostEstimate(flops=6 * 10**9, bytes_accessed=20 * 2**20, transcendentals=0),
        name="evolve",
    )(state, gates, moves, perms)


def body(amplitudes, gate_stack, targets):
    group = ("z", "lo")
    state = amplitudes.reshape(64, 16, 128)
    state = lax.all_to_all(state, group, split_axis=0, concat_axis=0, tiled=True)
    state = evolve(state, *prepare(targets, gate_stack))
    state = lax.all_to_all(state, group, split_axis=0, concat_axis=0, tiled=True)
    return state.reshape(amplitudes.shape)


def solution(mesh):
    split = Mesh(mesh.devices.reshape(2, 4, 16), ("top", "z", "lo"))
    in_specs = (P(("top", "z"), "lo", None), P(), P())
    out_specs = P(("top", "z"), "lo", None)
    return jax.shard_map(body, mesh=split, in_specs=in_specs, out_specs=out_specs, check_vma=False)
```

```python
import jax
import jax.numpy as jnp
from jax import lax
from jax.experimental import pallas as pl
from jax.experimental.pallas import tpu as pltpu
from jax.sharding import Mesh
from jax.sharding import PartitionSpec as P

LAYERS = 8
SPAN = 10
WIDE = 1 << SPAN
GATE = 128
FULL = WIDE - 1
LANES = GATE - 1
F32 = jnp.float32
BF16 = jnp.bfloat16
I32 = jnp.int32
PICKED = (7, 6, 7, 3)


def two_parts(value):
    high = value.astype(BF16)
    return high, (value - high.astype(F32)).astype(BF16)


def three_parts(value):
    high = value.astype(BF16)
    left = value - high.astype(F32)
    middle = left.astype(BF16)
    return high, middle, (left - middle.astype(F32)).astype(BF16)


def dot(left, right):
    return lax.dot_general(left, right, (((1,), (0,)), ((), ())), preferred_element_type=F32)


def left_form(parts):
    high, middle, low = parts
    return jnp.concatenate([high, middle], 1), jnp.concatenate([high, low], 1)


def right_form(parts):
    high, middle, low = parts
    both = jnp.concatenate([high, middle], 1)
    return jnp.concatenate([both, both], 0), jnp.concatenate([low, high], 0)


def full_dot(left, right):
    left, right = left_form(left), right_form(right)
    first = dot(left[0], right[0])
    return first[:, :GATE] + (first[:, GATE:] + dot(left[1], right[1]))


def lowest(mask, count):
    bits = []
    for _ in range(count):
        low = mask & -mask
        bits.append(low)
        mask = mask ^ low
    return bits


def union(bits):
    mask = bits[0]
    for bit in bits[1:]:
        mask = mask | bit
    return mask


def layer_orders(targets_ref):
    masks, tops = [LANES], [[128, 256, 512]]
    targets = []
    for layer in range(LAYERS):
        kind = layer % 4
        picked = [jnp.int32(1) << targets_ref[layer, j] for j in range(PICKED[kind])]
        targets.append(picked)
        mask = union(picked)
        other = FULL ^ mask
        if kind == 3:
            masks.append(other)
            tops.append(picked)
        else:
            masks.append(mask)
            tops.append(lowest(other, SPAN - PICKED[kind]))
    masks.append(LANES)
    tops.append([128, 256, 512])
    shared = [lowest(masks[s] & masks[s + 1], 3) for s in range(LAYERS + 1)]

    def order(stage, low):
        return low + lowest(masks[stage] ^ union(low), SPAN - 3 - len(tops[stage])) + tops[stage]

    taken = [None] + [order(s, shared[s - 1]) for s in range(1, LAYERS + 2)]
    left = [order(s, shared[s]) for s in range(LAYERS + 1)] + [None]
    return targets, taken, left


def spread(position, bits):
    value = jnp.zeros_like(position)
    for m, bit in enumerate(bits):
        value = jnp.where((position & (1 << m)) != 0, value + bit, value)
    return value


def collect(value, bits):
    position = jnp.zeros_like(value)
    for m, bit in enumerate(bits):
        position = jnp.where((value & bit) != 0, position + (1 << m), position)
    return position


def prepare_kernel(targets_ref, stack_ref, gates_ref, moves_ref, perms_ref, state, gram_ref, corners):
    lane = lax.broadcasted_iota(I32, (8, GATE), 1)
    targets, taken, left = layer_orders(targets_ref)
    for s in range(LAYERS + 1):
        source = collect(spread(lane, taken[s + 1][3:]), left[s][3:])
        moves_ref[s] = source * 8
    natural = [1 << m for m in range(7)]
    for i, (old, new) in enumerate(
        [(natural, left[0]), (taken[4], left[4]), (taken[8], left[8]), (taken[9], natural)]
    ):
        perms_ref[i] = collect(spread(lane, new[:7]), old[:7])
    row = lax.broadcasted_iota(I32, (GATE, GATE), 0)
    col = lax.broadcasted_iota(I32, (GATE, GATE), 1)
    ins, outs, deltas = [], [], []
    for g in range(LAYERS):
        vectors = stack_ref[g]
        lengths = jnp.sum(vectors * vectors, axis=1, keepdims=True)
        unit = vectors * lax.rsqrt(lengths)
        if g % 4 == 3:
            index_in = index_out = (lane & 15) << 3 | lane >> 4
        else:
            count = PICKED[g % 4]
            index_in, index_out = (
                collect(spread(lane, order[g + 1][:count]), targets[g]) + (lane >> count << count) for order in (taken, left)
            )
        pick_in = jnp.where(row == index_in[:1], 1.0, 0.0)
        pick_out = jnp.where(row == index_out[:1], 1.0, 0.0)
        out_rows = jnp.broadcast_to(index_out[:1], (GATE, GATE)).astype(F32).T
        deltas.append(jnp.where(out_rows == index_in[:1].astype(F32), 1.0, 0.0))
        parts = dot(jnp.concatenate(three_parts(unit), 0), jnp.concatenate([pick_in, pick_out], 1).astype(BF16))
        both = parts[:GATE] + parts[GATE : 2 * GATE] + parts[2 * GATE :]
        ins.append(three_parts(both[:, :GATE]))
        outs.append(both[:, GATE:].T)
        gram_ref[g] = full_dot(ins[g], three_parts(both[:, :GATE].T))
        for part in range(4):
            piece = gram_ref[g, 8 * part : 8 * part + 8, :]
            for b in range(1, 4):
                piece = jnp.where(lane >> 5 == b, gram_ref[g, 32 * b + 8 * part : 32 * b + 8 * part + 8, :], piece)
            corners[32 * g + 8 * part : 32 * g + 8 * part + 8, :] = piece
    solved = [None] * 32
    for k in range(31, -1, -1):
        entries = corners[pl.ds(k, 8, stride=32), :]

        def entry(j, entries=entries):
            return jnp.take_along_axis(entries, (lane & 96) | j, axis=1)

        total = jnp.where((lane & 31) == k, 1.0, 0.0)
        for j in range(31, k, -1):
            total = total - entry(j) * solved[j]
        solved[k] = total * (2.0 / entry(k))
    for k in range(32):
        corners[pl.ds(k, 8, stride=32), :] = solved[k]
    for g in range(LAYERS):
        for part in range(4):
            piece = corners[32 * g + 8 * part : 32 * g + 8 * part + 8, :]
            for b in range(4):
                state[g, 32 * b + 8 * part : 32 * b + 8 * part + 8, :] = jnp.where(lane >> 5 == b, piece, 0.0)
    for bit in (32, 64):
        upper = ((row & -(2 * bit)) == (col & -(2 * bit))) & ((col & bit) != 0) & ((row & bit) == 0)
        for g in range(LAYERS):
            now = state[g]
            now_parts = three_parts(now)
            first = full_dot(now_parts, three_parts(jnp.where(upper, gram_ref[g], 0.0)))
            state[g] = now - full_dot(three_parts(first), now_parts)
    for g in range(LAYERS):
        inner = full_dot(three_parts(state[g]), ins[g])
        gate = deltas[g] - full_dot(three_parts(outs[g]), three_parts(inner))
        if g % 4 == 1:
            gate = jnp.where(row < 64, gate, pltpu.roll(gate, 64, 1))
        high, low = two_parts(gate)
        gates_ref[g, :GATE, :] = jnp.concatenate([high, high], 1)
        gates_ref[g, GATE:, :] = jnp.concatenate([low, low], 1)


def prepare(targets, gate_stack):
    return pl.pallas_call(
        prepare_kernel,
        out_shape=(
            jax.ShapeDtypeStruct((LAYERS, 2 * GATE, 2 * GATE), BF16),
            jax.ShapeDtypeStruct((LAYERS + 1, 8, GATE), I32),
            jax.ShapeDtypeStruct((4, 8, GATE), I32),
        ),
        in_specs=[pl.BlockSpec(memory_space=pltpu.SMEM), pl.BlockSpec(memory_space=pltpu.VMEM)],
        out_specs=(pl.BlockSpec(memory_space=pltpu.VMEM),) * 3,
        scratch_shapes=[
            pltpu.VMEM((LAYERS, GATE, GATE), F32),
            pltpu.VMEM((LAYERS, GATE, GATE), F32),
            pltpu.VMEM((32 * LAYERS, GATE), F32),
        ],
        compiler_params=pltpu.CompilerParams(vmem_limit_bytes=24 * 2**20),
        cost_estimate=pl.CostEstimate(flops=8 * 10**9, bytes_accessed=20 * 2**20, transcendentals=0),
        name="prepare",
    )(targets, gate_stack)


def side_by_side(blocks):
    return jnp.concatenate([jnp.concatenate(block, 0) for block in blocks], 1)


def evolve_kernel(x_ref, gates_ref, moves_ref, perms_ref, out_ref, here, there, table, sem):
    copy = pltpu.make_async_copy(moves_ref, table, sem)
    copy.start()
    lane = lax.broadcasted_iota(I32, (64, GATE), 1)

    def permuted(value, i):
        return jnp.take_along_axis(value, jnp.broadcast_to(perms_ref[i, :1, :], value.shape), axis=1)

    for tile in range(8):
        value = jnp.concatenate([x_ref[:, tile, :], x_ref[:, 8 + tile, :]], 0)
        here[tile * GATE : (tile + 1) * GATE, :] = permuted(value, 0).T
    copy.wait()

    def rows(source, stage, first, count):
        return jnp.concatenate(
            [source[pl.ds(pl.multiple_of(table[stage, 0, first + i], 8), 8), :] for i in range(count)], 0
        )

    def applied(layer, blocks):
        out = dot(gates_ref[layer], side_by_side(blocks))
        return out[:GATE] + out[GATE:]

    source, target = here, there
    for layer in range(LAYERS):
        kind = layer % 4
        if kind == 1:
            width = 16 << (layer // 4)
            one = (lane & width) != 0
            for pair in range(8):
                blocks = []
                for i in range(2):
                    own = rows(source, layer, (2 * pair + i) * 8, 8)
                    other = jnp.where(one, pltpu.roll(own, width, 1), pltpu.roll(own, GATE - width, 1))
                    own, other = two_parts(own), two_parts(other)
                    blocks.append([own[0], other[0], own[1], other[1]])
                out = applied(layer, blocks)
                for i in range(2):
                    first = (2 * pair + i) * 64
                    part = out[:, GATE * i : GATE * (i + 1)]
                    target[first : first + 64, :] = jnp.where(one, part[64:], part[:64])
        elif kind == 3:
            tiles = [two_parts(rows(source, layer, tile * 16, 16).T) for tile in range(8)]
            outs = []
            for q in range(0, 8, 2):
                blocks = [
                    [tiles[t][part][16 * p : 16 * p + 16] for part in range(2) for t in range(8)] for p in (q, q + 1)
                ]
                outs.append(applied(layer, blocks))
            for tile in range(8):
                value = jnp.concatenate(
                    [outs[q // 2][16 * tile : 16 * tile + 16, GATE * (q % 2) : GATE * (q % 2 + 1)] for q in range(8)], 0
                )
                target[tile * GATE : (tile + 1) * GATE, :] = permuted(value, 1 + layer // 4).T
        else:
            for pair in range(4):
                blocks = [two_parts(rows(source, layer, (2 * pair + i) * 16, 16)) for i in range(2)]
                out = applied(layer, blocks)
                for i in range(2):
                    first = (2 * pair + i) * GATE
                    target[first : first + GATE, :] = out[:, GATE * i : GATE * (i + 1)]
        source, target = target, source
    for tile in range(8):
        value = permuted(rows(source, LAYERS, tile * 16, 16).T, 3)
        out_ref[:, tile, :] = value[:64]
        out_ref[:, 8 + tile, :] = value[64:]


def evolve(state, gates, moves, perms):
    return pl.pallas_call(
        evolve_kernel,
        out_shape=jax.ShapeDtypeStruct(state.shape, F32),
        in_specs=[pl.BlockSpec(memory_space=pltpu.VMEM)] * 4,
        out_specs=pl.BlockSpec(memory_space=pltpu.VMEM),
        scratch_shapes=[
            pltpu.VMEM((WIDE, GATE), F32),
            pltpu.VMEM((WIDE, GATE), F32),
            pltpu.SMEM((LAYERS + 1, 8, GATE), I32),
            pltpu.SemaphoreType.DMA,
        ],
        compiler_params=pltpu.CompilerParams(vmem_limit_bytes=24 * 2**20),
        cost_estimate=pl.CostEstimate(flops=6 * 10**9, bytes_accessed=20 * 2**20, transcendentals=0),
        name="evolve",
    )(state, gates, moves, perms)


def body(amplitudes, gate_stack, targets):
    group = ("z", "lo")
    state = amplitudes.reshape(64, 16, 128)
    state = lax.all_to_all(state, group, split_axis=0, concat_axis=0, tiled=True)
    state = evolve(state, *prepare(targets, gate_stack))
    state = lax.all_to_all(state, group, split_axis=0, concat_axis=0, tiled=True)
    return state.reshape(amplitudes.shape)


def solution(mesh):
    split = Mesh(mesh.devices.reshape(2, 4, 16), ("top", "z", "lo"))
    in_specs = (P(("top", "z"), "lo", None), P(), P())
    out_specs = P(("top", "z"), "lo", None)
    return jax.shard_map(body, mesh=split, in_specs=in_specs, out_specs=out_specs, check_vma=False)
```

```python
import jax
import jax.numpy as jnp
from jax import lax
from jax.experimental import pallas as pl
from jax.experimental.pallas import tpu as pltpu
from jax.sharding import Mesh
from jax.sharding import PartitionSpec as P

LAYERS = 8
SPAN = 10
WIDE = 1 << SPAN
GATE = 128
FULL = WIDE - 1
LANES = GATE - 1
F32 = jnp.float32
BF16 = jnp.bfloat16
I32 = jnp.int32
PICKED = (7, 6, 7, 3)


def two_parts(value):
    high = value.astype(BF16)
    return high, (value - high.astype(F32)).astype(BF16)


def three_parts(value):
    high = value.astype(BF16)
    left = value - high.astype(F32)
    middle = left.astype(BF16)
    return high, middle, (left - middle.astype(F32)).astype(BF16)


def dot(left, right):
    return lax.dot_general(left, right, (((1,), (0,)), ((), ())), preferred_element_type=F32)


def left_form(parts):
    high, middle, low = parts
    return jnp.concatenate([high, middle], 1), jnp.concatenate([high, low], 1)


def right_form(parts):
    high, middle, low = parts
    both = jnp.concatenate([high, middle], 1)
    return jnp.concatenate([both, both], 0), jnp.concatenate([low, high], 0)


def full_dot(left, right):
    left, right = left_form(left), right_form(right)
    first = dot(left[0], right[0])
    return first[:, :GATE] + (first[:, GATE:] + dot(left[1], right[1]))


def lowest(mask, count):
    bits = []
    for _ in range(count):
        low = mask & -mask
        bits.append(low)
        mask = mask ^ low
    return bits


def union(bits):
    mask = bits[0]
    for bit in bits[1:]:
        mask = mask | bit
    return mask


def layer_orders(targets_ref):
    masks, tops = [LANES], [[128, 256, 512]]
    targets = []
    for layer in range(LAYERS):
        kind = layer % 4
        picked = [jnp.int32(1) << targets_ref[layer, j] for j in range(PICKED[kind])]
        targets.append(picked)
        mask = union(picked)
        other = FULL ^ mask
        if kind == 3:
            masks.append(other)
            tops.append(picked)
        else:
            masks.append(mask)
            tops.append(lowest(other, SPAN - PICKED[kind]))
    masks.append(LANES)
    tops.append([128, 256, 512])
    shared = [lowest(masks[s] & masks[s + 1], 3) for s in range(LAYERS + 1)]

    def order(stage, low):
        return low + lowest(masks[stage] ^ union(low), SPAN - 3 - len(tops[stage])) + tops[stage]

    taken = [None] + [order(s, shared[s - 1]) for s in range(1, LAYERS + 2)]
    left = [order(s, shared[s]) for s in range(LAYERS + 1)] + [None]
    return targets, taken, left


def spread(position, bits):
    value = jnp.zeros_like(position)
    for m, bit in enumerate(bits):
        value = jnp.where((position & (1 << m)) != 0, value + bit, value)
    return value


def collect(value, bits):
    position = jnp.zeros_like(value)
    for m, bit in enumerate(bits):
        position = jnp.where((value & bit) != 0, position + (1 << m), position)
    return position


def prepare_kernel(targets_ref, stack_ref, gates_ref, moves_ref, picks_ref, state, gram_ref, corners):
    lane = lax.broadcasted_iota(I32, (8, GATE), 1)
    targets, taken, left = layer_orders(targets_ref)
    shift = jnp.zeros_like(lane)
    for m in range(1, 7):
        shift = jnp.where(lane == 1 << m, 3 * m, shift)
    for s in range(LAYERS + 1):
        source = collect(spread(lane, taken[s + 1][3:]), left[s][3:])
        place = jnp.zeros_like(lane)
        for p in range(1, 7):
            place = jnp.where(source == 1 << p, p, place)
        code = jnp.where((lane & (lane - 1)) == 0, place << shift, 0)
        code = jnp.sum(code.astype(F32), axis=1, keepdims=True)
        moves_ref[pl.ds(s, 1), :] = jnp.broadcast_to(code[:1].astype(I32), (1, GATE))
    natural = [1 << m for m in range(7)]
    perms = []
    for i, (old, new) in enumerate(
        [(natural, left[0]), (taken[4], left[4]), (taken[8], left[8]), (taken[9], natural)]
    ):
        perms.append(collect(spread(lane, new[:7]), old[:7])[:1].astype(F32))
    row = lax.broadcasted_iota(I32, (GATE, GATE), 0)
    col = lax.broadcasted_iota(I32, (GATE, GATE), 1)
    for i, perm in enumerate(perms):
        perm = jnp.broadcast_to(perm, (GATE, GATE))
        picks_ref[i] = jnp.where((perm if i == 3 else perm.T) == (row if i == 3 else col).astype(F32), 1.0, 0.0).astype(BF16)
    ins, outs, deltas = [], [], []
    for g in range(LAYERS):
        vectors = stack_ref[g]
        lengths = jnp.sum(vectors * vectors, axis=1, keepdims=True)
        unit = vectors * lax.rsqrt(lengths)
        if g % 4 == 3:
            index_in = index_out = (lane & 15) << 3 | lane >> 4
        else:
            count = PICKED[g % 4]
            index_in, index_out = (
                collect(spread(lane, order[g + 1][:count]), targets[g]) + (lane >> count << count) for order in (taken, left)
            )
        pick_in = jnp.where(row == index_in[:1], 1.0, 0.0)
        pick_out = jnp.where(row == index_out[:1], 1.0, 0.0)
        out_rows = jnp.broadcast_to(index_out[:1], (GATE, GATE)).astype(F32).T
        deltas.append(jnp.where(out_rows == index_in[:1].astype(F32), 1.0, 0.0))
        parts = dot(jnp.concatenate(three_parts(unit), 0), jnp.concatenate([pick_in, pick_out], 1).astype(BF16))
        both = parts[:GATE] + parts[GATE : 2 * GATE] + parts[2 * GATE :]
        ins.append(three_parts(both[:, :GATE]))
        outs.append(both[:, GATE:].T)
        gram_ref[g] = full_dot(ins[g], three_parts(both[:, :GATE].T))
        for part in range(4):
            piece = gram_ref[g, 8 * part : 8 * part + 8, :]
            for b in range(1, 4):
                piece = jnp.where(lane >> 5 == b, gram_ref[g, 32 * b + 8 * part : 32 * b + 8 * part + 8, :], piece)
            corners[32 * g + 8 * part : 32 * g + 8 * part + 8, :] = piece
    solved = [None] * 32
    for k in range(31, -1, -1):
        entries = corners[pl.ds(k, 8, stride=32), :]

        def entry(j, entries=entries):
            return jnp.take_along_axis(entries, (lane & 96) | j, axis=1)

        total = jnp.where((lane & 31) == k, 1.0, 0.0)
        for j in range(31, k, -1):
            total = total - entry(j) * solved[j]
        solved[k] = total * (2.0 / entry(k))
    for k in range(32):
        corners[pl.ds(k, 8, stride=32), :] = solved[k]
    for g in range(LAYERS):
        for part in range(4):
            piece = corners[32 * g + 8 * part : 32 * g + 8 * part + 8, :]
            for b in range(4):
                state[g, 32 * b + 8 * part : 32 * b + 8 * part + 8, :] = jnp.where(lane >> 5 == b, piece, 0.0)
    for bit in (32, 64):
        upper = ((row & -(2 * bit)) == (col & -(2 * bit))) & ((col & bit) != 0) & ((row & bit) == 0)
        for g in range(LAYERS):
            now = state[g]
            now_parts = three_parts(now)
            first = full_dot(now_parts, three_parts(jnp.where(upper, gram_ref[g], 0.0)))
            state[g] = now - full_dot(three_parts(first), now_parts)
    for g in range(LAYERS):
        inner = full_dot(three_parts(state[g]), ins[g])
        gate = deltas[g] - full_dot(three_parts(outs[g]), three_parts(inner))
        if g % 4 == 1:
            gate = jnp.where(row < 64, gate, pltpu.roll(gate, 64, 1))
        high, low = two_parts(gate)
        gates_ref[g, :GATE, :] = jnp.concatenate([high, high], 1)
        gates_ref[g, GATE:, :] = jnp.concatenate([low, low], 1)


def prepare(targets, gate_stack):
    return pl.pallas_call(
        prepare_kernel,
        out_shape=(
            jax.ShapeDtypeStruct((LAYERS, 2 * GATE, 2 * GATE), BF16),
            jax.ShapeDtypeStruct((16, GATE), I32),
            jax.ShapeDtypeStruct((4, GATE, GATE), BF16),
        ),
        in_specs=[pl.BlockSpec(memory_space=pltpu.SMEM), pl.BlockSpec(memory_space=pltpu.VMEM)],
        out_specs=(pl.BlockSpec(memory_space=pltpu.VMEM),) * 3,
        scratch_shapes=[
            pltpu.VMEM((LAYERS, GATE, GATE), F32),
            pltpu.VMEM((LAYERS, GATE, GATE), F32),
            pltpu.VMEM((32 * LAYERS, GATE), F32),
        ],
        compiler_params=pltpu.CompilerParams(vmem_limit_bytes=24 * 2**20),
        cost_estimate=pl.CostEstimate(flops=8 * 10**9, bytes_accessed=20 * 2**20, transcendentals=0),
        name="prepare",
    )(targets, gate_stack)


def side_by_side(blocks):
    return jnp.concatenate([jnp.concatenate(block, 0) for block in blocks], 1)


def sums(steps):
    values = [jnp.int32(0)]
    for step in steps:
        values += [value + step for value in values]
    return values


def evolve_kernel(x_ref, gates_ref, moves_ref, picks_ref, out_ref, here, there):
    lane = lax.broadcasted_iota(I32, (64, GATE), 1)

    def turned(pick, parts):
        return lax.dot_general(pick, jnp.concatenate(parts, 0), (((1,), (1,)), ((), ())), preferred_element_type=F32)

    def turned_sum(pick, value):
        out = turned(pick, two_parts(value))
        return out[:, :GATE] + out[:, GATE:]

    for tile in range(8):
        value = jnp.concatenate([x_ref[:, tile, :], x_ref[:, 8 + tile, :]], 0)
        here[tile * GATE : (tile + 1) * GATE, :] = turned_sum(picks_ref[0], value)
    firsts = []
    codes = [moves_ref[stage, 0] for stage in range(LAYERS + 1)]
    for stage in range(LAYERS + 1):
        code = codes[stage]
        steps = [jnp.int32(8) << ((code >> (3 * m)) & 7) for m in range(7)]
        firsts.append((sums(steps[:4]), sums(steps[4:])))

    def rows(source, stage, first, count):
        low, high = firsts[stage]
        places = [high[(first + i) // 16] + low[(first + i) % 16] for i in range(count)]
        return jnp.concatenate([source[pl.ds(pl.multiple_of(place, 8), 8), :] for place in places], 0)

    def applied(layer, blocks):
        out = dot(gates_ref[layer], side_by_side(blocks))
        return out[:GATE] + out[GATE:]

    source, target = here, there
    for layer in range(LAYERS):
        kind = layer % 4
        if kind == 1:
            width = 16 << (layer // 4)
            one = (lane & width) != 0
            partner = lane ^ width
            for pair in range(8):
                blocks = []
                for i in range(2):
                    own = rows(source, layer, (2 * pair + i) * 8, 8)
                    other = jnp.take_along_axis(own, partner, axis=1)
                    own, other = two_parts(own), two_parts(other)
                    blocks.append([own[0], other[0], own[1], other[1]])
                out = applied(layer, blocks)
                for i in range(2):
                    first = (2 * pair + i) * 64
                    part = out[:, GATE * i : GATE * (i + 1)]
                    target[first : first + 64, :] = jnp.where(one, part[64:], part[:64])
        elif kind == 3:
            tiles = [two_parts(rows(source, layer, tile * 16, 16).T) for tile in range(8)]
            outs = []
            for q in range(0, 8, 2):
                blocks = [
                    [tiles[t][part][16 * p : 16 * p + 16] for part in range(2) for t in range(8)] for p in (q, q + 1)
                ]
                outs.append(applied(layer, blocks))
            for tile in range(8):
                value = jnp.concatenate(
                    [outs[q // 2][16 * tile : 16 * tile + 16, GATE * (q % 2) : GATE * (q % 2 + 1)] for q in range(8)], 0
                )
                target[tile * GATE : (tile + 1) * GATE, :] = turned_sum(picks_ref[1 + layer // 4], value)
        else:
            blocks = [two_parts(rows(source, layer, i * 16, 16)) for i in range(8)]
            out = applied(layer, blocks)
            for i in range(8):
                target[i * GATE : (i + 1) * GATE, :] = out[:, GATE * i : GATE * (i + 1)]
        source, target = target, source
    last = jnp.concatenate([picks_ref[3]] * 2, 0)
    for tile in range(8):
        value = rows(source, LAYERS, tile * 16, 16).T
        high, low = two_parts(value)
        value = dot(jnp.concatenate([high, low], 1), last)
        out_ref[:, tile, :] = value[:64]
        out_ref[:, 8 + tile, :] = value[64:]


def evolve(state, gates, moves, perms):
    return pl.pallas_call(
        evolve_kernel,
        out_shape=jax.ShapeDtypeStruct(state.shape, F32),
        in_specs=[pl.BlockSpec(memory_space=pltpu.VMEM)] * 4,
        out_specs=pl.BlockSpec(memory_space=pltpu.VMEM),
        scratch_shapes=[
            pltpu.VMEM((WIDE, GATE), F32),
            pltpu.VMEM((WIDE, GATE), F32),
        ],
        compiler_params=pltpu.CompilerParams(vmem_limit_bytes=24 * 2**20),
        cost_estimate=pl.CostEstimate(flops=6 * 10**9, bytes_accessed=20 * 2**20, transcendentals=0),
        name="evolve",
    )(state, gates, moves, perms)


def body(amplitudes, gate_stack, targets):
    group = ("z", "lo")
    state = amplitudes.reshape(64, 16, 128)
    state = lax.all_to_all(state, group, split_axis=0, concat_axis=0, tiled=True)
    state = evolve(state, *prepare(targets, gate_stack))
    state = lax.all_to_all(state, group, split_axis=0, concat_axis=0, tiled=True)
    return state.reshape(amplitudes.shape)


def solution(mesh):
    split = Mesh(mesh.devices.reshape(2, 4, 16), ("top", "z", "lo"))
    in_specs = (P(("top", "z"), "lo", None), P(), P())
    out_specs = P(("top", "z"), "lo", None)
    return jax.shard_map(body, mesh=split, in_specs=in_specs, out_specs=out_specs, check_vma=False)
```

```python
import jax
import jax.numpy as jnp
from jax import lax
from jax.experimental import pallas as pl
from jax.experimental.pallas import tpu as pltpu
from jax.sharding import Mesh
from jax.sharding import PartitionSpec as P

LAYERS = 8
SPAN = 10
WIDE = 1 << SPAN
GATE = 128
FULL = WIDE - 1
LANES = GATE - 1
F32 = jnp.float32
BF16 = jnp.bfloat16
I32 = jnp.int32
PICKED = (7, 6, 7, 3)


def two_parts(value):
    high = value.astype(BF16)
    return high, (value - high.astype(F32)).astype(BF16)


def three_parts(value):
    high = value.astype(BF16)
    left = value - high.astype(F32)
    middle = left.astype(BF16)
    return high, middle, (left - middle.astype(F32)).astype(BF16)


def dot(left, right):
    return lax.dot_general(left, right, (((1,), (0,)), ((), ())), preferred_element_type=F32)


def left_form(parts):
    high, middle, low = parts
    return jnp.concatenate([high, middle], 1), jnp.concatenate([high, low], 1)


def right_form(parts):
    high, middle, low = parts
    both = jnp.concatenate([high, middle], 1)
    return jnp.concatenate([both, both], 0), jnp.concatenate([low, high], 0)


def full_dot(left, right):
    left, right = left_form(left), right_form(right)
    first = dot(left[0], right[0])
    return first[:, :GATE] + (first[:, GATE:] + dot(left[1], right[1]))


def lowest(mask, count):
    bits = []
    for _ in range(count):
        low = mask & -mask
        bits.append(low)
        mask = mask ^ low
    return bits


def union(bits):
    mask = bits[0]
    for bit in bits[1:]:
        mask = mask | bit
    return mask


def layer_orders(targets_ref):
    masks, tops = [LANES], [[128, 256, 512]]
    targets = []
    for layer in range(LAYERS):
        kind = layer % 4
        picked = [jnp.int32(1) << targets_ref[layer, j] for j in range(PICKED[kind])]
        targets.append(picked)
        mask = union(picked)
        other = FULL ^ mask
        if kind == 3:
            masks.append(other)
            tops.append(picked)
        else:
            masks.append(mask)
            tops.append(lowest(other, SPAN - PICKED[kind]))
    masks.append(LANES)
    tops.append([128, 256, 512])
    shared = [lowest(masks[s] & masks[s + 1], 3) for s in range(LAYERS + 1)]

    def order(stage, low):
        return low + lowest(masks[stage] ^ union(low), SPAN - 3 - len(tops[stage])) + tops[stage]

    taken = [None] + [order(s, shared[s - 1]) for s in range(1, LAYERS + 2)]
    left = [order(s, shared[s]) for s in range(LAYERS + 1)] + [None]
    return targets, taken, left


def spread(position, bits):
    value = jnp.zeros_like(position)
    for m, bit in enumerate(bits):
        value = jnp.where((position & (1 << m)) != 0, value + bit, value)
    return value


def collect(value, bits):
    position = jnp.zeros_like(value)
    for m, bit in enumerate(bits):
        position = jnp.where((value & bit) != 0, position + (1 << m), position)
    return position


def prepare_kernel(targets_ref, stack_ref, gates_ref, moves_ref, picks_ref, state, gram_ref, corners):
    lane = lax.broadcasted_iota(I32, (8, GATE), 1)
    targets, taken, left = layer_orders(targets_ref)
    shift = jnp.zeros_like(lane)
    for m in range(1, 7):
        shift = jnp.where(lane == 1 << m, 3 * m, shift)
    for s in range(LAYERS + 1):
        source = collect(spread(lane, taken[s + 1][3:]), left[s][3:])
        place = jnp.zeros_like(lane)
        for p in range(1, 7):
            place = jnp.where(source == 1 << p, p, place)
        code = jnp.where((lane & (lane - 1)) == 0, place << shift, 0)
        code = jnp.sum(code.astype(F32), axis=1, keepdims=True)
        moves_ref[pl.ds(s, 1), :] = jnp.broadcast_to(code[:1].astype(I32), (1, GATE))
    natural = [1 << m for m in range(7)]
    perms = []
    for i, (old, new) in enumerate(
        [(natural, left[0]), (taken[4], left[4]), (taken[8], left[8]), (taken[9], natural)]
    ):
        perms.append(collect(spread(lane, new[:7]), old[:7])[:1].astype(F32))
    row = lax.broadcasted_iota(I32, (GATE, GATE), 0)
    col = lax.broadcasted_iota(I32, (GATE, GATE), 1)
    for i, perm in enumerate(perms):
        perm = jnp.broadcast_to(perm, (GATE, GATE))
        picks_ref[i] = jnp.where((perm if i == 3 else perm.T) == (row if i == 3 else col).astype(F32), 1.0, 0.0).astype(BF16)
    tall = lax.broadcasted_iota(I32, (2 * GATE, GATE), 0)
    picks_in, picks_out = [], []
    for g in range(LAYERS):
        if g % 4 == 3:
            index_in = index_out = (lane & 15) << 3 | lane >> 4
        else:
            count = PICKED[g % 4]
            index_in, index_out = (
                collect(spread(lane, order[g + 1][:count]), targets[g]) + (lane >> count << count) for order in (taken, left)
            )
        picks_in.append(jnp.where(row == index_in[:1], 1.0, 0.0).astype(BF16))
        picks_out.append(jnp.where(row == index_out[:1], 1.0, 0.0).T.astype(BF16))
    units, units_t = [], []
    for g in range(LAYERS):
        vectors = stack_ref[g]
        lengths = jnp.sum(vectors * vectors, axis=1, keepdims=True)
        unit = vectors * lax.rsqrt(lengths)
        units.append(three_parts(unit))
        units_t.append(three_parts(unit.T))
        gram_ref[g] = full_dot(units[g], units_t[g])
        for part in range(4):
            piece = gram_ref[g, 8 * part : 8 * part + 8, :]
            for b in range(1, 4):
                piece = jnp.where(lane >> 5 == b, gram_ref[g, 32 * b + 8 * part : 32 * b + 8 * part + 8, :], piece)
            corners[32 * g + 8 * part : 32 * g + 8 * part + 8, :] = piece
    solved = [None] * 32
    for k in range(31, -1, -1):
        entries = corners[pl.ds(k, 8, stride=32), :]

        def entry(j, entries=entries):
            return jnp.take_along_axis(entries, (lane & 96) | j, axis=1)

        total = jnp.where((lane & 31) == k, 1.0, 0.0)
        for j in range(31, k, -1):
            total = total - entry(j) * solved[j]
        solved[k] = total * (2.0 / entry(k))
    for k in range(32):
        corners[pl.ds(k, 8, stride=32), :] = solved[k]
    for g in range(LAYERS):
        for part in range(4):
            piece = corners[32 * g + 8 * part : 32 * g + 8 * part + 8, :]
            for b in range(4):
                state[g, 32 * b + 8 * part : 32 * b + 8 * part + 8, :] = jnp.where(lane >> 5 == b, piece, 0.0)
    for bit in (32, 64):
        upper = ((row & -(2 * bit)) == (col & -(2 * bit))) & ((col & bit) != 0) & ((row & bit) == 0)
        halves = [slice(first, first + bit) for first in range(0, GATE, 2 * bit)]
        firsts = []
        for g in range(LAYERS):
            top = jnp.concatenate([state[g, half, :] for half in halves], 0)
            firsts.append(full_dot(three_parts(top), three_parts(jnp.where(upper, gram_ref[g], 0.0))))
        for g in range(LAYERS):
            change = full_dot(three_parts(firsts[g]), three_parts(state[g]))
            for i, half in enumerate(halves):
                state[g, half, :] = state[g, half, :] - change[bit * i : bit * (i + 1)]
    inners = [full_dot(three_parts(state[g]), units[g]) for g in range(LAYERS)]
    gates = [
        jnp.where(row == col, 1.0, 0.0) - full_dot(units_t[g], three_parts(inners[g])) for g in range(LAYERS)
    ]
    moved = []
    for g in range(LAYERS):
        moved.append(dot(picks_out[g], jnp.concatenate(two_parts(gates[g]), 1)).astype(BF16))
    for g in range(LAYERS):
        parts = dot(jnp.concatenate([moved[g][:, :GATE], moved[g][:, GATE:]], 0), picks_in[g])
        if g % 4 == 1:
            parts = jnp.where((tall & 64) == 0, parts, pltpu.roll(parts, 64, 1))
        parts = parts.astype(BF16)
        gates_ref[g] = jnp.concatenate([parts, parts], 1)


def prepare(targets, gate_stack):
    return pl.pallas_call(
        prepare_kernel,
        out_shape=(
            jax.ShapeDtypeStruct((LAYERS, 2 * GATE, 2 * GATE), BF16),
            jax.ShapeDtypeStruct((16, GATE), I32),
            jax.ShapeDtypeStruct((4, GATE, GATE), BF16),
        ),
        in_specs=[pl.BlockSpec(memory_space=pltpu.SMEM), pl.BlockSpec(memory_space=pltpu.VMEM)],
        out_specs=(pl.BlockSpec(memory_space=pltpu.VMEM),) * 3,
        scratch_shapes=[
            pltpu.VMEM((LAYERS, GATE, GATE), F32),
            pltpu.VMEM((LAYERS, GATE, GATE), F32),
            pltpu.VMEM((32 * LAYERS, GATE), F32),
        ],
        compiler_params=pltpu.CompilerParams(vmem_limit_bytes=24 * 2**20),
        cost_estimate=pl.CostEstimate(flops=8 * 10**9, bytes_accessed=20 * 2**20, transcendentals=0),
        name="prepare",
    )(targets, gate_stack)


def side_by_side(blocks):
    return jnp.concatenate([jnp.concatenate(block, 0) for block in blocks], 1)


def sums(steps):
    values = [jnp.int32(0)]
    for step in steps:
        values += [value + step for value in values]
    return values


def evolve_kernel(x_ref, gates_ref, moves_ref, picks_ref, out_ref, here, there):
    lane = lax.broadcasted_iota(I32, (64, GATE), 1)

    def turned(pick, parts):
        return lax.dot_general(pick, jnp.concatenate(parts, 0), (((1,), (1,)), ((), ())), preferred_element_type=F32)

    def turned_sum(pick, value):
        out = turned(pick, two_parts(value))
        return out[:, :GATE] + out[:, GATE:]

    values = [jnp.concatenate([x_ref[:, tile, :], x_ref[:, 8 + tile, :]], 0) for tile in range(8)]
    values = [turned_sum(picks_ref[0], value) for value in values]
    for tile in range(8):
        here[tile * GATE : (tile + 1) * GATE, :] = values[tile]
    firsts = []
    codes = [moves_ref[stage, 0] for stage in range(LAYERS + 1)]
    for stage in range(LAYERS + 1):
        code = codes[stage]
        steps = [jnp.int32(8) << ((code >> (3 * m)) & 7) for m in range(7)]
        firsts.append((sums(steps[:4]), sums(steps[4:])))

    def rows(source, stage, first, count):
        low, high = firsts[stage]
        places = [high[(first + i) // 16] + low[(first + i) % 16] for i in range(count)]
        return jnp.concatenate([source[pl.ds(pl.multiple_of(place, 8), 8), :] for place in places], 0)

    def applied(layer, blocks):
        out = dot(gates_ref[layer], side_by_side(blocks))
        return out[:GATE] + out[GATE:]

    source, target = here, there
    for layer in range(LAYERS):
        kind = layer % 4
        if kind == 1:
            width = 16 << (layer // 4)
            one = (lane & width) != 0
            partner = lane ^ width
            blocks = []
            for i in range(16):
                own = rows(source, layer, i * 8, 8)
                other = jnp.take_along_axis(own, partner, axis=1)
                own, other = two_parts(own), two_parts(other)
                blocks.append([own[0], other[0], own[1], other[1]])
            out = applied(layer, blocks)
            for i in range(16):
                part = out[:, GATE * i : GATE * (i + 1)]
                target[i * 64 : (i + 1) * 64, :] = jnp.where(one, part[64:], part[:64])
        elif kind == 3:
            tiles = [rows(source, layer, tile * 16, 16) for tile in range(8)]
            tiles = [two_parts(tile.T) for tile in tiles]
            outs = []
            for q in range(0, 8, 2):
                blocks = [
                    [tiles[t][part][16 * p : 16 * p + 16] for part in range(2) for t in range(8)] for p in (q, q + 1)
                ]
                outs.append(applied(layer, blocks))
            values = []
            for tile in range(8):
                value = jnp.concatenate(
                    [outs[q // 2][16 * tile : 16 * tile + 16, GATE * (q % 2) : GATE * (q % 2 + 1)] for q in range(8)], 0
                )
                values.append(turned_sum(picks_ref[1 + layer // 4], value))
            for tile in range(8):
                target[tile * GATE : (tile + 1) * GATE, :] = values[tile]
        else:
            blocks = [two_parts(rows(source, layer, i * 16, 16)) for i in range(8)]
            out = applied(layer, blocks)
            for i in range(8):
                target[i * GATE : (i + 1) * GATE, :] = out[:, GATE * i : GATE * (i + 1)]
        source, target = target, source
    last = jnp.concatenate([picks_ref[3]] * 2, 0)
    values = [rows(source, LAYERS, tile * 16, 16) for tile in range(8)]
    values = [dot(jnp.concatenate(two_parts(value.T), 1), last) for value in values]
    for tile in range(8):
        out_ref[:, tile, :] = values[tile][:64]
        out_ref[:, 8 + tile, :] = values[tile][64:]


def evolve(state, gates, moves, perms):
    return pl.pallas_call(
        evolve_kernel,
        out_shape=jax.ShapeDtypeStruct(state.shape, F32),
        in_specs=[pl.BlockSpec(memory_space=pltpu.VMEM)] * 4,
        out_specs=pl.BlockSpec(memory_space=pltpu.VMEM),
        scratch_shapes=[
            pltpu.VMEM((WIDE, GATE), F32),
            pltpu.VMEM((WIDE, GATE), F32),
        ],
        compiler_params=pltpu.CompilerParams(vmem_limit_bytes=24 * 2**20),
        cost_estimate=pl.CostEstimate(flops=6 * 10**9, bytes_accessed=20 * 2**20, transcendentals=0),
        name="evolve",
    )(state, gates, moves, perms)


def body(amplitudes, gate_stack, targets):
    group = ("z", "lo")
    state = amplitudes.reshape(64, 16, 128)
    state = lax.all_to_all(state, group, split_axis=0, concat_axis=0, tiled=True)
    state = evolve(state, *prepare(targets, gate_stack))
    state = lax.all_to_all(state, group, split_axis=0, concat_axis=0, tiled=True)
    return state.reshape(amplitudes.shape)


def solution(mesh):
    split = Mesh(mesh.devices.reshape(2, 4, 16), ("top", "z", "lo"))
    in_specs = (P(("top", "z"), "lo", None), P(), P())
    out_specs = P(("top", "z"), "lo", None)
    return jax.shard_map(body, mesh=split, in_specs=in_specs, out_specs=out_specs, check_vma=False)
```

```python
import jax
import jax.numpy as jnp
from jax import lax
from jax.experimental import pallas as pl
from jax.experimental.pallas import tpu as pltpu
from jax.sharding import Mesh
from jax.sharding import PartitionSpec as P

LAYERS = 8
SPAN = 10
WIDE = 1 << SPAN
GATE = 128
FULL = WIDE - 1
LANES = GATE - 1
F32 = jnp.float32
BF16 = jnp.bfloat16
I32 = jnp.int32
PICKED = (7, 6, 7, 3)


def two_parts(value):
    high = value.astype(BF16)
    return high, (value - high.astype(F32)).astype(BF16)


def three_parts(value):
    high = value.astype(BF16)
    left = value - high.astype(F32)
    middle = left.astype(BF16)
    return high, middle, (left - middle.astype(F32)).astype(BF16)


def dot(left, right):
    return lax.dot_general(left, right, (((1,), (0,)), ((), ())), preferred_element_type=F32)


def left_form(parts):
    high, middle, low = parts
    return jnp.concatenate([high, middle], 1), jnp.concatenate([high, low], 1)


def right_form(parts):
    high, middle, low = parts
    both = jnp.concatenate([high, middle], 1)
    return jnp.concatenate([both, both], 0), jnp.concatenate([low, high], 0)


def full_dot(left, right):
    left, right = left_form(left), right_form(right)
    first = dot(left[0], right[0])
    return first[:, :GATE] + (first[:, GATE:] + dot(left[1], right[1]))


def lowest(mask, count):
    bits = []
    for _ in range(count):
        low = mask & -mask
        bits.append(low)
        mask = mask ^ low
    return bits


def union(bits):
    mask = bits[0]
    for bit in bits[1:]:
        mask = mask | bit
    return mask


def layer_orders(targets_ref):
    masks, tops = [LANES], [[128, 256, 512]]
    targets = []
    for layer in range(LAYERS):
        kind = layer % 4
        picked = [jnp.int32(1) << targets_ref[layer, j] for j in range(PICKED[kind])]
        targets.append(picked)
        mask = union(picked)
        other = FULL ^ mask
        if kind == 3:
            masks.append(other)
            tops.append(picked)
        else:
            masks.append(mask)
            tops.append(lowest(other, SPAN - PICKED[kind]))
    masks.append(LANES)
    tops.append([128, 256, 512])
    shared = [lowest(masks[s] & masks[s + 1], 3) for s in range(LAYERS + 1)]

    def order(stage, low):
        return low + lowest(masks[stage] ^ union(low), SPAN - 3 - len(tops[stage])) + tops[stage]

    taken = [None] + [order(s, shared[s - 1]) for s in range(1, LAYERS + 2)]
    left = [order(s, shared[s]) for s in range(LAYERS + 1)] + [None]
    return targets, taken, left


def spread(position, bits):
    value = jnp.zeros_like(position)
    for m, bit in enumerate(bits):
        value = jnp.where((position & (1 << m)) != 0, value + bit, value)
    return value


def collect(value, bits):
    position = jnp.zeros_like(value)
    for m, bit in enumerate(bits):
        position = jnp.where((value & bit) != 0, position + (1 << m), position)
    return position


def prepare_kernel(targets_ref, stack_ref, gates_ref, moves_ref, picks_ref, state, gram_ref, corners):
    lane = lax.broadcasted_iota(I32, (8, GATE), 1)
    targets, taken, left = layer_orders(targets_ref)
    shift = jnp.zeros_like(lane)
    for m in range(1, 7):
        shift = jnp.where(lane == 1 << m, 3 * m, shift)
    for s in range(LAYERS + 1):
        source = collect(spread(lane, taken[s + 1][3:]), left[s][3:])
        place = jnp.zeros_like(lane)
        for p in range(1, 7):
            place = jnp.where(source == 1 << p, p, place)
        code = jnp.where((lane & (lane - 1)) == 0, place << shift, 0)
        code = jnp.sum(code.astype(F32), axis=1, keepdims=True)
        moves_ref[pl.ds(s, 1), :] = jnp.broadcast_to(code[:1].astype(I32), (1, GATE))
    natural = [1 << m for m in range(7)]
    perms = []
    for i, (old, new) in enumerate(
        [(natural, left[0]), (taken[4], left[4]), (taken[8], left[8]), (taken[9], natural)]
    ):
        perms.append(collect(spread(lane, new[:7]), old[:7])[:1].astype(F32))
    row = lax.broadcasted_iota(I32, (GATE, GATE), 0)
    col = lax.broadcasted_iota(I32, (GATE, GATE), 1)
    for i, perm in enumerate(perms):
        perm = jnp.broadcast_to(perm, (GATE, GATE))
        picks_ref[i] = jnp.where((perm if i == 3 else perm.T) == (row if i == 3 else col).astype(F32), 1.0, 0.0).astype(BF16)
    tall = lax.broadcasted_iota(I32, (2 * GATE, GATE), 0)
    picks_in, picks_out = [], []
    for g in range(LAYERS):
        if g % 4 == 3:
            index_in = index_out = (lane & 15) << 3 | lane >> 4
        else:
            count = PICKED[g % 4]
            index_in, index_out = (
                collect(spread(lane, order[g + 1][:count]), targets[g]) + (lane >> count << count) for order in (taken, left)
            )
        picks_in.append(jnp.where(row == index_in[:1], 1.0, 0.0).astype(BF16))
        picks_out.append(jnp.where(row == index_out[:1], 1.0, 0.0).T.astype(BF16))
    units, units_t = [], []
    for g in range(LAYERS):
        vectors = stack_ref[g]
        lengths = jnp.sum(vectors * vectors, axis=1, keepdims=True)
        unit = vectors * lax.rsqrt(lengths)
        units.append(three_parts(unit))
        units_t.append(three_parts(unit.T))
        gram_ref[g] = full_dot(units[g], units_t[g])
        for part in range(4):
            piece = gram_ref[g, 8 * part : 8 * part + 8, :]
            for b in range(1, 4):
                piece = jnp.where(lane >> 5 == b, gram_ref[g, 32 * b + 8 * part : 32 * b + 8 * part + 8, :], piece)
            corners[32 * g + 8 * part : 32 * g + 8 * part + 8, :] = piece
    solved = [None] * 32
    for k in range(31, -1, -1):
        entries = corners[pl.ds(k, 8, stride=32), :]

        def entry(j, entries=entries):
            return jnp.take_along_axis(entries, (lane & 96) | j, axis=1)

        total = jnp.where((lane & 31) == k, 1.0, 0.0)
        for j in range(31, k, -1):
            total = total - entry(j) * solved[j]
        solved[k] = total * (2.0 / entry(k))
    for k in range(32):
        corners[pl.ds(k, 8, stride=32), :] = solved[k]
    for g in range(LAYERS):
        for part in range(4):
            piece = corners[32 * g + 8 * part : 32 * g + 8 * part + 8, :]
            for b in range(4):
                state[g, 32 * b + 8 * part : 32 * b + 8 * part + 8, :] = jnp.where(lane >> 5 == b, piece, 0.0)
    for bit in (32, 64):
        upper = ((row & -(2 * bit)) == (col & -(2 * bit))) & ((col & bit) != 0) & ((row & bit) == 0)
        halves = [slice(first, first + bit) for first in range(0, GATE, 2 * bit)]
        firsts = []
        for g in range(LAYERS):
            top = jnp.concatenate([state[g, half, :] for half in halves], 0)
            firsts.append(full_dot(three_parts(top), three_parts(jnp.where(upper, gram_ref[g], 0.0))))
        for g in range(LAYERS):
            change = full_dot(three_parts(firsts[g]), three_parts(state[g]))
            for i, half in enumerate(halves):
                state[g, half, :] = state[g, half, :] - change[bit * i : bit * (i + 1)]
    inners = [full_dot(three_parts(state[g]), units[g]) for g in range(LAYERS)]
    gates = [
        jnp.where(row == col, 1.0, 0.0) - full_dot(units_t[g], three_parts(inners[g])) for g in range(LAYERS)
    ]
    moved = []
    for g in range(LAYERS):
        moved.append(dot(picks_out[g], jnp.concatenate(two_parts(gates[g]), 1)).astype(BF16))
    for g in range(LAYERS):
        parts = dot(jnp.concatenate([moved[g][:, :GATE], moved[g][:, GATE:]], 0), picks_in[g])
        if g % 4 == 1:
            parts = jnp.where((tall & 64) == 0, parts, pltpu.roll(parts, 64, 1))
        parts = parts.astype(BF16)
        gates_ref[g] = jnp.concatenate([parts, parts], 1)


def prepare(targets, gate_stack):
    return pl.pallas_call(
        prepare_kernel,
        out_shape=(
            jax.ShapeDtypeStruct((LAYERS, 2 * GATE, 2 * GATE), BF16),
            jax.ShapeDtypeStruct((16, GATE), I32),
            jax.ShapeDtypeStruct((4, GATE, GATE), BF16),
        ),
        in_specs=[pl.BlockSpec(memory_space=pltpu.SMEM), pl.BlockSpec(memory_space=pltpu.VMEM)],
        out_specs=(pl.BlockSpec(memory_space=pltpu.VMEM),) * 3,
        scratch_shapes=[
            pltpu.VMEM((LAYERS, GATE, GATE), F32),
            pltpu.VMEM((LAYERS, GATE, GATE), F32),
            pltpu.VMEM((32 * LAYERS, GATE), F32),
        ],
        compiler_params=pltpu.CompilerParams(vmem_limit_bytes=24 * 2**20),
        cost_estimate=pl.CostEstimate(flops=8 * 10**9, bytes_accessed=20 * 2**20, transcendentals=0),
        name="prepare",
    )(targets, gate_stack)


def side_by_side(blocks):
    return jnp.concatenate([jnp.concatenate(block, 0) for block in blocks], 1)


def sums(steps):
    values = [jnp.int32(0)]
    for step in steps:
        values += [value + step for value in values]
    return values


def evolve_kernel(core_ref, x_ref, gates_ref, moves_ref, picks_ref, out_ref, send_ref, here, there, ends):
    lane = lax.broadcasted_iota(I32, (64, GATE), 1)

    def turned(pick, parts):
        return lax.dot_general(pick, jnp.concatenate(parts, 0), (((1,), (1,)), ((), ())), preferred_element_type=F32)

    def turned_sum(pick, value):
        out = turned(pick, two_parts(value))
        return out[:, :GATE] + out[:, GATE:]

    values = [jnp.concatenate([x_ref[:, tile, :], x_ref[:, 8 + tile, :]], 0) for tile in range(8)]
    values = [turned_sum(picks_ref[0], value) for value in values]
    for tile in range(8):
        here[tile * GATE : (tile + 1) * GATE, :] = values[tile]
    firsts = []
    codes = [moves_ref[stage, 0] for stage in range(LAYERS + 1)]
    for stage in range(LAYERS + 1):
        code = codes[stage]
        steps = [jnp.int32(8) << ((code >> (3 * m)) & 7) for m in range(7)]
        firsts.append((sums(steps[:4]), sums(steps[4:])))

    def rows(source, stage, first, count):
        low, high = firsts[stage]
        places = [high[(first + i) // 16] + low[(first + i) % 16] for i in range(count)]
        return jnp.concatenate([source[pl.ds(pl.multiple_of(place, 8), 8), :] for place in places], 0)

    def applied(layer, blocks):
        out = dot(gates_ref[layer], side_by_side(blocks))
        return out[:GATE] + out[GATE:]

    source, target = here, there
    for layer in range(LAYERS):
        kind = layer % 4
        if kind == 1:
            width = 16 << (layer // 4)
            one = (lane & width) != 0
            partner = lane ^ width
            blocks = []
            for i in range(16):
                own = rows(source, layer, i * 8, 8)
                other = jnp.take_along_axis(own, partner, axis=1)
                own, other = two_parts(own), two_parts(other)
                blocks.append([own[0], other[0], own[1], other[1]])
            out = applied(layer, blocks)
            for i in range(16):
                part = out[:, GATE * i : GATE * (i + 1)]
                target[i * 64 : (i + 1) * 64, :] = jnp.where(one, part[64:], part[:64])
        elif kind == 3:
            tiles = [rows(source, layer, tile * 16, 16) for tile in range(8)]
            tiles = [two_parts(tile.T) for tile in tiles]
            outs = []
            for q in range(0, 8, 2):
                blocks = [
                    [tiles[t][part][16 * p : 16 * p + 16] for part in range(2) for t in range(8)] for p in (q, q + 1)
                ]
                outs.append(applied(layer, blocks))
            values = []
            for tile in range(8):
                value = jnp.concatenate(
                    [outs[q // 2][16 * tile : 16 * tile + 16, GATE * (q % 2) : GATE * (q % 2 + 1)] for q in range(8)], 0
                )
                values.append(turned_sum(picks_ref[1 + layer // 4], value))
            for tile in range(8):
                target[tile * GATE : (tile + 1) * GATE, :] = values[tile]
        else:
            blocks = [two_parts(rows(source, layer, i * 16, 16)) for i in range(8)]
            out = applied(layer, blocks)
            for i in range(8):
                target[i * GATE : (i + 1) * GATE, :] = out[:, GATE * i : GATE * (i + 1)]
        source, target = target, source
    last = jnp.concatenate([picks_ref[3]] * 2, 0)
    values = [rows(source, LAYERS, tile * 16, 16) for tile in range(8)]
    values = [dot(jnp.concatenate(two_parts(value.T), 1), last) for value in values]
    for tile in range(8):
        ends[:, tile, :] = values[tile][:64]
        ends[:, 8 + tile, :] = values[tile][64:]
    core = core_ref[0]
    for pair in range(32):
        out_ref[pair, core] = ends[2 * pair + core]
        send_ref[pair] = ends[2 * pair + 1 - core]


def evolve(core, state, gates, moves, perms):
    return pl.pallas_call(
        evolve_kernel,
        out_shape=(
            jax.ShapeDtypeStruct((32, 2, 16, GATE), F32),
            jax.ShapeDtypeStruct((32, 16, GATE), F32),
        ),
        in_specs=[pl.BlockSpec(memory_space=pltpu.SMEM)] + [pl.BlockSpec(memory_space=pltpu.VMEM)] * 4,
        out_specs=(pl.BlockSpec(memory_space=pltpu.VMEM),) * 2,
        scratch_shapes=[
            pltpu.VMEM((WIDE, GATE), F32),
            pltpu.VMEM((WIDE, GATE), F32),
            pltpu.VMEM((64, 16, GATE), F32),
        ],
        compiler_params=pltpu.CompilerParams(vmem_limit_bytes=24 * 2**20),
        cost_estimate=pl.CostEstimate(flops=6 * 10**9, bytes_accessed=20 * 2**20, transcendentals=0),
        name="evolve",
    )(core, state, gates, moves, perms)


def body(amplitudes, gate_stack, targets):
    core = lax.axis_index("core").astype(I32)
    state = amplitudes.reshape(64, 16, 128)
    state = lax.all_to_all(state, ("z", "yx", "core"), split_axis=0, concat_axis=0, tiled=True)
    kept, sent = evolve(core[None], state, *prepare(targets, gate_stack))
    got = lax.ppermute(sent, "core", [(0, 1), (1, 0)])
    state = lax.dynamic_update_slice_in_dim(kept, got[:, None], 1 - core, 1)
    state = lax.all_to_all(state, ("z", "yx"), split_axis=0, concat_axis=0, tiled=True)
    return state.reshape(amplitudes.shape)


def solution(mesh):
    split = Mesh(mesh.devices.reshape(2, 4, 8, 2), ("top", "z", "yx", "core"))
    place = P(("top", "z"), ("yx", "core"), None)
    return jax.shard_map(body, mesh=split, in_specs=(place, P(), P()), out_specs=place, check_vma=False)
```

```python
import jax
import jax.numpy as jnp
from jax import lax
from jax.experimental import pallas as pl
from jax.experimental.pallas import tpu as pltpu
from jax.sharding import Mesh
from jax.sharding import PartitionSpec as P

LAYERS = 8
SPAN = 10
WIDE = 1 << SPAN
GATE = 128
FULL = WIDE - 1
LANES = GATE - 1
F32 = jnp.float32
BF16 = jnp.bfloat16
I32 = jnp.int32
PICKED = (7, 6, 7, 3)


def two_parts(value):
    high = value.astype(BF16)
    return high, (value - high.astype(F32)).astype(BF16)


def three_parts(value):
    high = value.astype(BF16)
    left = value - high.astype(F32)
    middle = left.astype(BF16)
    return high, middle, (left - middle.astype(F32)).astype(BF16)


def dot(left, right):
    return lax.dot_general(left, right, (((1,), (0,)), ((), ())), preferred_element_type=F32)


def left_form(parts):
    high, middle, low = parts
    return jnp.concatenate([high, middle], 1), jnp.concatenate([high, low], 1)


def right_form(parts):
    high, middle, low = parts
    both = jnp.concatenate([high, middle], 1)
    return jnp.concatenate([both, both], 0), jnp.concatenate([low, high], 0)


def full_dot(left, right):
    left, right = left_form(left), right_form(right)
    first = dot(left[0], right[0])
    return first[:, :GATE] + (first[:, GATE:] + dot(left[1], right[1]))


def lowest(mask, count):
    bits = []
    for _ in range(count):
        low = mask & -mask
        bits.append(low)
        mask = mask ^ low
    return bits


def union(bits):
    mask = bits[0]
    for bit in bits[1:]:
        mask = mask | bit
    return mask


def layer_orders(targets_ref):
    masks, tops = [LANES], [[128, 256, 512]]
    targets = []
    for layer in range(LAYERS):
        kind = layer % 4
        picked = [jnp.int32(1) << targets_ref[layer, j] for j in range(PICKED[kind])]
        targets.append(picked)
        mask = union(picked)
        other = FULL ^ mask
        if kind == 3:
            masks.append(other)
            tops.append(picked)
        else:
            masks.append(mask)
            tops.append(lowest(other, SPAN - PICKED[kind]))
    masks.append(LANES)
    tops.append([128, 256, 512])
    shared = [lowest(masks[s] & masks[s + 1], 3) for s in range(LAYERS + 1)]

    def order(stage, low):
        return low + lowest(masks[stage] ^ union(low), SPAN - 3 - len(tops[stage])) + tops[stage]

    taken = [None] + [order(s, shared[s - 1]) for s in range(1, LAYERS + 2)]
    left = [order(s, shared[s]) for s in range(LAYERS + 1)] + [None]
    return targets, taken, left


def spread(position, bits):
    value = jnp.zeros_like(position)
    for m, bit in enumerate(bits):
        value = jnp.where((position & (1 << m)) != 0, value + bit, value)
    return value


def collect(value, bits):
    position = jnp.zeros_like(value)
    for m, bit in enumerate(bits):
        position = jnp.where((value & bit) != 0, position + (1 << m), position)
    return position


def prepare_kernel(targets_ref, stack_ref, gates_ref, moves_ref, picks_ref, state, gram_ref, corners):
    lane = lax.broadcasted_iota(I32, (8, GATE), 1)
    targets, taken, left = layer_orders(targets_ref)
    shift = jnp.zeros_like(lane)
    for m in range(1, 7):
        shift = jnp.where(lane == 1 << m, 3 * m, shift)
    for s in range(LAYERS + 1):
        source = collect(spread(lane, taken[s + 1][3:]), left[s][3:])
        place = jnp.zeros_like(lane)
        for p in range(1, 7):
            place = jnp.where(source == 1 << p, p, place)
        code = jnp.where((lane & (lane - 1)) == 0, place << shift, 0)
        code = jnp.sum(code.astype(F32), axis=1, keepdims=True)
        moves_ref[pl.ds(s, 1), :] = jnp.broadcast_to(code[:1].astype(I32), (1, GATE))
    natural = [1 << m for m in range(7)]
    perms = []
    for i, (old, new) in enumerate(
        [(natural, left[0]), (taken[4], left[4]), (taken[8], left[8]), (taken[9], natural)]
    ):
        perms.append(collect(spread(lane, new[:7]), old[:7])[:1].astype(F32))
    row = lax.broadcasted_iota(I32, (GATE, GATE), 0)
    col = lax.broadcasted_iota(I32, (GATE, GATE), 1)
    for i, perm in enumerate(perms):
        perm = jnp.broadcast_to(perm, (GATE, GATE))
        picks_ref[i] = jnp.where((perm if i == 3 else perm.T) == (row if i == 3 else col).astype(F32), 1.0, 0.0).astype(BF16)
    tall = lax.broadcasted_iota(I32, (2 * GATE, GATE), 0)
    picks_in, picks_out = [], []
    for g in range(LAYERS):
        if g % 4 == 3:
            index_in = index_out = (lane & 15) << 3 | lane >> 4
        else:
            count = PICKED[g % 4]
            index_in, index_out = (
                collect(spread(lane, order[g + 1][:count]), targets[g]) + (lane >> count << count) for order in (taken, left)
            )
        picks_in.append(jnp.where(row == index_in[:1], 1.0, 0.0).astype(BF16))
        picks_out.append(jnp.where(row == index_out[:1], 1.0, 0.0).T.astype(BF16))
    units, units_t = [], []
    for g in range(LAYERS):
        vectors = stack_ref[g]
        lengths = jnp.sum(vectors * vectors, axis=1, keepdims=True)
        unit = vectors * lax.rsqrt(lengths)
        units.append(three_parts(unit))
        units_t.append(three_parts(unit.T))
        gram_ref[g] = full_dot(units[g], units_t[g])
        for part in range(4):
            piece = gram_ref[g, 8 * part : 8 * part + 8, :]
            for b in range(1, 4):
                piece = jnp.where(lane >> 5 == b, gram_ref[g, 32 * b + 8 * part : 32 * b + 8 * part + 8, :], piece)
            corners[32 * g + 8 * part : 32 * g + 8 * part + 8, :] = piece
    solved = [None] * 32
    for k in range(31, -1, -1):
        entries = corners[pl.ds(k, 8, stride=32), :]

        def entry(j, entries=entries):
            return jnp.take_along_axis(entries, (lane & 96) | j, axis=1)

        total = jnp.where((lane & 31) == k, 1.0, 0.0)
        for j in range(31, k, -1):
            total = total - entry(j) * solved[j]
        solved[k] = total * (2.0 / entry(k))
    for k in range(32):
        corners[pl.ds(k, 8, stride=32), :] = solved[k]
    for g in range(LAYERS):
        for part in range(4):
            piece = corners[32 * g + 8 * part : 32 * g + 8 * part + 8, :]
            for b in range(4):
                state[g, 32 * b + 8 * part : 32 * b + 8 * part + 8, :] = jnp.where(lane >> 5 == b, piece, 0.0)
    for bit in (32, 64):
        upper = ((row & -(2 * bit)) == (col & -(2 * bit))) & ((col & bit) != 0) & ((row & bit) == 0)
        halves = [slice(first, first + bit) for first in range(0, GATE, 2 * bit)]
        firsts = []
        for g in range(LAYERS):
            top = jnp.concatenate([state[g, half, :] for half in halves], 0)
            firsts.append(full_dot(three_parts(top), three_parts(jnp.where(upper, gram_ref[g], 0.0))))
        for g in range(LAYERS):
            change = full_dot(three_parts(firsts[g]), three_parts(state[g]))
            for i, half in enumerate(halves):
                state[g, half, :] = state[g, half, :] - change[bit * i : bit * (i + 1)]
    inners = [full_dot(three_parts(state[g]), units[g]) for g in range(LAYERS)]
    gates = [
        jnp.where(row == col, 1.0, 0.0) - full_dot(units_t[g], three_parts(inners[g])) for g in range(LAYERS)
    ]
    moved = []
    for g in range(LAYERS):
        moved.append(dot(picks_out[g], jnp.concatenate(two_parts(gates[g]), 1)).astype(BF16))
    for g in range(LAYERS):
        parts = dot(jnp.concatenate([moved[g][:, :GATE], moved[g][:, GATE:]], 0), picks_in[g])
        if g % 4 == 1:
            parts = jnp.where((tall & 64) == 0, parts, pltpu.roll(parts, 64, 1))
        parts = parts.astype(BF16)
        gates_ref[g] = jnp.concatenate([parts[:GATE], parts[:GATE], parts[GATE:]], 1)


def prepare(targets, gate_stack):
    return pl.pallas_call(
        prepare_kernel,
        out_shape=(
            jax.ShapeDtypeStruct((LAYERS, GATE, 3 * GATE), BF16),
            jax.ShapeDtypeStruct((16, GATE), I32),
            jax.ShapeDtypeStruct((4, GATE, GATE), BF16),
        ),
        in_specs=[pl.BlockSpec(memory_space=pltpu.SMEM), pl.BlockSpec(memory_space=pltpu.VMEM)],
        out_specs=(pl.BlockSpec(memory_space=pltpu.VMEM),) * 3,
        scratch_shapes=[
            pltpu.VMEM((LAYERS, GATE, GATE), F32),
            pltpu.VMEM((LAYERS, GATE, GATE), F32),
            pltpu.VMEM((32 * LAYERS, GATE), F32),
        ],
        compiler_params=pltpu.CompilerParams(vmem_limit_bytes=24 * 2**20),
        cost_estimate=pl.CostEstimate(flops=8 * 10**9, bytes_accessed=20 * 2**20, transcendentals=0),
        name="prepare",
    )(targets, gate_stack)


def side_by_side(blocks):
    return jnp.concatenate([jnp.concatenate(block, 0) for block in blocks], 1)


def sums(steps):
    values = [jnp.int32(0)]
    for step in steps:
        values += [value + step for value in values]
    return values


def evolve_kernel(core_ref, x_ref, gates_ref, moves_ref, picks_ref, out_ref, send_ref, here, there, ends):
    lane = lax.broadcasted_iota(I32, (64, GATE), 1)

    def turned_sum(pick, value):
        return lax.dot_general(
            jnp.concatenate([pick, pick], 1),
            jnp.concatenate(two_parts(value), 1),
            (((1,), (1,)), ((), ())),
            preferred_element_type=F32,
        )

    values = [jnp.concatenate([x_ref[:, tile, :], x_ref[:, 8 + tile, :]], 0) for tile in range(8)]
    values = [turned_sum(picks_ref[0], value) for value in values]
    for tile in range(8):
        here[tile * GATE : (tile + 1) * GATE, :] = values[tile]
    firsts = []
    codes = [moves_ref[stage, 0] for stage in range(LAYERS + 1)]
    for stage in range(LAYERS + 1):
        code = codes[stage]
        steps = [jnp.int32(8) << ((code >> (3 * m)) & 7) for m in range(7)]
        firsts.append((sums(steps[:4]), sums(steps[4:])))

    def rows(source, stage, first, count):
        low, high = firsts[stage]
        places = [high[(first + i) // 16] + low[(first + i) % 16] for i in range(count)]
        return jnp.concatenate([source[pl.ds(pl.multiple_of(place, 8), 8), :] for place in places], 0)

    def applied(layer, blocks):
        stacked = side_by_side(blocks)
        return dot(gates_ref[layer], jnp.concatenate([stacked, stacked[:GATE]], 0))

    source, target = here, there
    for layer in range(LAYERS):
        kind = layer % 4
        if kind == 1:
            width = 16 << (layer // 4)
            one = (lane & width) != 0
            partner = lane ^ width
            blocks = []
            for i in range(16):
                own = rows(source, layer, i * 8, 8)
                other = jnp.take_along_axis(own, partner, axis=1)
                own, other = two_parts(own), two_parts(other)
                blocks.append([own[0], other[0], own[1], other[1]])
            out = applied(layer, blocks)
            for i in range(16):
                part = out[:, GATE * i : GATE * (i + 1)]
                target[i * 64 : (i + 1) * 64, :] = jnp.where(one, part[64:], part[:64])
        elif kind == 3:
            tiles = [rows(source, layer, tile * 16, 16) for tile in range(8)]
            tiles = [two_parts(tile.T) for tile in tiles]
            outs = []
            for q in range(0, 8, 2):
                blocks = [
                    [tiles[t][part][16 * p : 16 * p + 16] for part in range(2) for t in range(8)] for p in (q, q + 1)
                ]
                outs.append(applied(layer, blocks))
            values = []
            for tile in range(8):
                value = jnp.concatenate(
                    [outs[q // 2][16 * tile : 16 * tile + 16, GATE * (q % 2) : GATE * (q % 2 + 1)] for q in range(8)], 0
                )
                values.append(turned_sum(picks_ref[1 + layer // 4], value))
            for tile in range(8):
                target[tile * GATE : (tile + 1) * GATE, :] = values[tile]
        else:
            blocks = [two_parts(rows(source, layer, i * 16, 16)) for i in range(8)]
            out = applied(layer, blocks)
            for i in range(8):
                target[i * GATE : (i + 1) * GATE, :] = out[:, GATE * i : GATE * (i + 1)]
        source, target = target, source
    last = jnp.concatenate([picks_ref[3]] * 2, 0)
    values = [rows(source, LAYERS, tile * 16, 16) for tile in range(8)]
    values = [dot(jnp.concatenate(two_parts(value.T), 1), last) for value in values]
    for tile in range(8):
        ends[:, tile, :] = values[tile][:64]
        ends[:, 8 + tile, :] = values[tile][64:]
    core = core_ref[0]
    for pair in range(32):
        out_ref[pair, core] = ends[2 * pair + core]
        send_ref[pair] = ends[2 * pair + 1 - core]


def evolve(core, state, gates, moves, perms):
    return pl.pallas_call(
        evolve_kernel,
        out_shape=(
            jax.ShapeDtypeStruct((32, 2, 16, GATE), F32),
            jax.ShapeDtypeStruct((32, 16, GATE), F32),
        ),
        in_specs=[pl.BlockSpec(memory_space=pltpu.SMEM)] + [pl.BlockSpec(memory_space=pltpu.VMEM)] * 4,
        out_specs=(pl.BlockSpec(memory_space=pltpu.VMEM),) * 2,
        scratch_shapes=[
            pltpu.VMEM((WIDE, GATE), F32),
            pltpu.VMEM((WIDE, GATE), F32),
            pltpu.VMEM((64, 16, GATE), F32),
        ],
        compiler_params=pltpu.CompilerParams(vmem_limit_bytes=24 * 2**20),
        cost_estimate=pl.CostEstimate(flops=6 * 10**9, bytes_accessed=20 * 2**20, transcendentals=0),
        name="evolve",
    )(core, state, gates, moves, perms)


def body(amplitudes, gate_stack, targets):
    core = lax.axis_index("core").astype(I32)
    state = amplitudes.reshape(64, 16, 128)
    state = lax.all_to_all(state, ("z", "yx", "core"), split_axis=0, concat_axis=0, tiled=True)
    kept, sent = evolve(core[None], state, *prepare(targets, gate_stack))
    got = lax.ppermute(sent, "core", [(0, 1), (1, 0)])
    state = lax.dynamic_update_slice_in_dim(kept, got[:, None], 1 - core, 1)
    state = lax.all_to_all(state, ("z", "yx"), split_axis=0, concat_axis=0, tiled=True)
    return state.reshape(amplitudes.shape)


def solution(mesh):
    split = Mesh(mesh.devices.reshape(2, 4, 8, 2), ("top", "z", "yx", "core"))
    place = P(("top", "z"), ("yx", "core"), None)
    return jax.shard_map(body, mesh=split, in_specs=(place, P(), P()), out_specs=place, check_vma=False)
```

```python
import jax
import jax.numpy as jnp
from jax import lax
from jax.experimental import pallas as pl
from jax.experimental.pallas import tpu as pltpu
from jax.sharding import Mesh
from jax.sharding import PartitionSpec as P

LAYERS = 8
SPAN = 10
WIDE = 1 << SPAN
GATE = 128
FULL = WIDE - 1
LANES = GATE - 1
F32 = jnp.float32
BF16 = jnp.bfloat16
I32 = jnp.int32
PICKED = (7, 6, 7, 3)


def two_parts(value):
    high = value.astype(BF16)
    return high, (value - high.astype(F32)).astype(BF16)


def three_parts(value):
    high = value.astype(BF16)
    left = value - high.astype(F32)
    middle = left.astype(BF16)
    return high, middle, (left - middle.astype(F32)).astype(BF16)


def dot(left, right):
    return lax.dot_general(left, right, (((1,), (0,)), ((), ())), preferred_element_type=F32)


def left_form(parts):
    high, middle, low = parts
    return jnp.concatenate([high, middle], 1), jnp.concatenate([high, low], 1)


def right_form(parts):
    high, middle, low = parts
    both = jnp.concatenate([high, middle], 1)
    return jnp.concatenate([both, both], 0), jnp.concatenate([low, high], 0)


def full_dot(left, right):
    left, right = left_form(left), right_form(right)
    first = dot(left[0], right[0])
    return first[:, :GATE] + (first[:, GATE:] + dot(left[1], right[1]))


def lowest(mask, count):
    bits = []
    for _ in range(count):
        low = mask & -mask
        bits.append(low)
        mask = mask ^ low
    return bits


def union(bits):
    mask = bits[0]
    for bit in bits[1:]:
        mask = mask | bit
    return mask


def layer_orders(targets_ref):
    masks, tops = [LANES], [[128, 256, 512]]
    targets = []
    for layer in range(LAYERS):
        kind = layer % 4
        picked = [jnp.int32(1) << targets_ref[layer, j] for j in range(PICKED[kind])]
        targets.append(picked)
        mask = union(picked)
        other = FULL ^ mask
        if kind == 3:
            masks.append(other)
            tops.append(picked)
        else:
            masks.append(mask)
            tops.append(lowest(other, SPAN - PICKED[kind]))
    masks.append(LANES)
    tops.append([128, 256, 512])
    shared = [lowest(masks[s] & masks[s + 1], 3) for s in range(LAYERS + 1)]

    def order(stage, low):
        return low + lowest(masks[stage] ^ union(low), SPAN - 3 - len(tops[stage])) + tops[stage]

    taken = [None] + [order(s, shared[s - 1]) for s in range(1, LAYERS + 2)]
    left = [order(s, shared[s]) for s in range(LAYERS + 1)] + [None]
    return targets, taken, left


def spread(position, bits):
    value = jnp.zeros_like(position)
    for m, bit in enumerate(bits):
        value = jnp.where((position & (1 << m)) != 0, value + bit, value)
    return value


def collect(value, bits):
    position = jnp.zeros_like(value)
    for m, bit in enumerate(bits):
        position = jnp.where((value & bit) != 0, position + (1 << m), position)
    return position


def prepare_kernel(targets_ref, stack_ref, gates_ref, moves_ref, picks_ref, state, gram_ref, corners):
    lane = lax.broadcasted_iota(I32, (8, GATE), 1)
    targets, taken, left = layer_orders(targets_ref)
    shift = jnp.zeros_like(lane)
    for m in range(1, 7):
        shift = jnp.where(lane == 1 << m, 3 * m, shift)
    for s in range(LAYERS + 1):
        source = collect(spread(lane, taken[s + 1][3:]), left[s][3:])
        place = jnp.zeros_like(lane)
        for p in range(1, 7):
            place = jnp.where(source == 1 << p, p, place)
        code = jnp.where((lane & (lane - 1)) == 0, place << shift, 0)
        code = jnp.sum(code.astype(F32), axis=1, keepdims=True)
        moves_ref[pl.ds(s, 1), :] = jnp.broadcast_to(code[:1].astype(I32), (1, GATE))
    natural = [1 << m for m in range(7)]
    perms = []
    for i, (old, new) in enumerate(
        [(natural, left[0]), (taken[4], left[4]), (taken[8], left[8]), (taken[9], natural)]
    ):
        perms.append(collect(spread(lane, new[:7]), old[:7])[:1].astype(F32))
    row = lax.broadcasted_iota(I32, (GATE, GATE), 0)
    col = lax.broadcasted_iota(I32, (GATE, GATE), 1)
    for i, perm in enumerate(perms):
        perm = jnp.broadcast_to(perm, (GATE, GATE))
        picks_ref[i] = jnp.where((perm if i == 3 else perm.T) == (row if i == 3 else col).astype(F32), 1.0, 0.0).astype(BF16)
    tall = lax.broadcasted_iota(I32, (2 * GATE, GATE), 0)
    picks_in, picks_out = [], []
    for g in range(LAYERS):
        if g % 4 == 3:
            index_in = index_out = (lane & 15) << 3 | lane >> 4
        else:
            count = PICKED[g % 4]
            index_in, index_out = (
                collect(spread(lane, order[g + 1][:count]), targets[g]) + (lane >> count << count) for order in (taken, left)
            )
        picks_in.append(jnp.where(row == index_in[:1], 1.0, 0.0).astype(BF16))
        picks_out.append(jnp.where(row == index_out[:1], 1.0, 0.0).T.astype(BF16))
    units, units_t = [], []
    for g in range(LAYERS):
        vectors = stack_ref[g]
        lengths = jnp.sum(vectors * vectors, axis=1, keepdims=True)
        unit = vectors * lax.rsqrt(lengths)
        units.append(three_parts(unit))
        units_t.append(three_parts(unit.T))
        gram_ref[g] = full_dot(units[g], units_t[g])
        for part in range(4):
            piece = gram_ref[g, 8 * part : 8 * part + 8, :]
            for b in range(1, 4):
                piece = jnp.where(lane >> 5 == b, gram_ref[g, 32 * b + 8 * part : 32 * b + 8 * part + 8, :], piece)
            corners[32 * g + 8 * part : 32 * g + 8 * part + 8, :] = piece
    solved = [None] * 32
    for k in range(31, -1, -1):
        entries = corners[pl.ds(k, 8, stride=32), :]

        def entry(j, entries=entries):
            return jnp.take_along_axis(entries, (lane & 96) | j, axis=1)

        total = jnp.where((lane & 31) == k, 1.0, 0.0)
        for j in range(31, k, -1):
            total = total - entry(j) * solved[j]
        solved[k] = total * (2.0 / entry(k))
    for k in range(32):
        corners[pl.ds(k, 8, stride=32), :] = solved[k]
    for g in range(LAYERS):
        for part in range(4):
            piece = corners[32 * g + 8 * part : 32 * g + 8 * part + 8, :]
            for b in range(4):
                state[g, 32 * b + 8 * part : 32 * b + 8 * part + 8, :] = jnp.where(lane >> 5 == b, piece, 0.0)
    for bit in (32, 64):
        upper = ((row & -(2 * bit)) == (col & -(2 * bit))) & ((col & bit) != 0) & ((row & bit) == 0)
        halves = [slice(first, first + bit) for first in range(0, GATE, 2 * bit)]
        firsts = []
        for g in range(LAYERS):
            top = jnp.concatenate([state[g, half, :] for half in halves], 0)
            firsts.append(full_dot(three_parts(top), three_parts(jnp.where(upper, gram_ref[g], 0.0))))
        for g in range(LAYERS):
            change = full_dot(three_parts(firsts[g]), three_parts(state[g]))
            for i, half in enumerate(halves):
                state[g, half, :] = state[g, half, :] - change[bit * i : bit * (i + 1)]
    inners = [full_dot(three_parts(state[g]), units[g]) for g in range(LAYERS)]
    gates = [
        jnp.where(row == col, 1.0, 0.0) - full_dot(units_t[g], three_parts(inners[g])) for g in range(LAYERS)
    ]
    moved = []
    for g in range(LAYERS):
        moved.append(dot(picks_out[g], jnp.concatenate(two_parts(gates[g]), 1)).astype(BF16))
    for g in range(LAYERS):
        parts = dot(jnp.concatenate([moved[g][:, :GATE], moved[g][:, GATE:]], 0), picks_in[g])
        if g % 4 == 1:
            parts = jnp.where((tall & 64) == 0, parts, pltpu.roll(parts, 64, 1))
        parts = parts.astype(BF16)
        gates_ref[g] = jnp.concatenate([parts, parts], 1)


def prepare(targets, gate_stack):
    return pl.pallas_call(
        prepare_kernel,
        out_shape=(
            jax.ShapeDtypeStruct((LAYERS, 2 * GATE, 2 * GATE), BF16),
            jax.ShapeDtypeStruct((16, GATE), I32),
            jax.ShapeDtypeStruct((4, GATE, GATE), BF16),
        ),
        in_specs=[pl.BlockSpec(memory_space=pltpu.SMEM), pl.BlockSpec(memory_space=pltpu.VMEM)],
        out_specs=(pl.BlockSpec(memory_space=pltpu.VMEM),) * 3,
        scratch_shapes=[
            pltpu.VMEM((LAYERS, GATE, GATE), F32),
            pltpu.VMEM((LAYERS, GATE, GATE), F32),
            pltpu.VMEM((32 * LAYERS, GATE), F32),
        ],
        compiler_params=pltpu.CompilerParams(vmem_limit_bytes=24 * 2**20),
        cost_estimate=pl.CostEstimate(flops=8 * 10**9, bytes_accessed=20 * 2**20, transcendentals=0),
        name="prepare",
    )(targets, gate_stack)


def side_by_side(blocks):
    return jnp.concatenate([jnp.concatenate(block, 0) for block in blocks], 1)


def sums(steps):
    values = [jnp.int32(0)]
    for step in steps:
        values += [value + step for value in values]
    return values


def evolve_kernel(core_ref, x_ref, gates_ref, moves_ref, picks_ref, out_ref, send_ref, here, there, ends):
    lane = lax.broadcasted_iota(I32, (64, GATE), 1)

    def turned_sum(pick, value):
        return lax.dot_general(
            jnp.concatenate([pick, pick], 1),
            jnp.concatenate(two_parts(value), 1),
            (((1,), (1,)), ((), ())),
            preferred_element_type=F32,
        )

    values = [jnp.concatenate([x_ref[:, tile, :], x_ref[:, 8 + tile, :]], 0) for tile in range(8)]
    values = [turned_sum(picks_ref[0], value) for value in values]
    for tile in range(8):
        here[tile * GATE : (tile + 1) * GATE, :] = values[tile]
    firsts = []
    codes = [moves_ref[stage, 0] for stage in range(LAYERS + 1)]
    for stage in range(LAYERS + 1):
        code = codes[stage]
        steps = [jnp.int32(8) << ((code >> (3 * m)) & 7) for m in range(7)]
        firsts.append((sums(steps[:4]), sums(steps[4:])))

    def rows(source, stage, first, count):
        low, high = firsts[stage]
        places = [high[(first + i) // 16] + low[(first + i) % 16] for i in range(count)]
        return jnp.concatenate([source[pl.ds(pl.multiple_of(place, 8), 8), :] for place in places], 0)

    def applied(layer, blocks):
        out = dot(gates_ref[layer], side_by_side(blocks))
        return out[:GATE] + out[GATE:]

    source, target = here, there
    for layer in range(LAYERS):
        kind = layer % 4
        if kind == 1:
            width = 16 << (layer // 4)
            one = (lane & width) != 0
            partner = lane ^ width
            blocks = []
            for i in range(16):
                own = rows(source, layer, i * 8, 8)
                other = jnp.take_along_axis(own, partner, axis=1)
                own, other = two_parts(own), two_parts(other)
                blocks.append([own[0], other[0], own[1], other[1]])
            out = applied(layer, blocks)
            for i in range(16):
                part = out[:, GATE * i : GATE * (i + 1)]
                target[i * 64 : (i + 1) * 64, :] = jnp.where(one, part[64:], part[:64])
        elif kind == 3:
            tiles = [rows(source, layer, tile * 16, 16) for tile in range(8)]
            tiles = [two_parts(tile.T) for tile in tiles]
            outs = []
            for q in range(0, 8, 2):
                blocks = [
                    [tiles[t][part][16 * p : 16 * p + 16] for part in range(2) for t in range(8)] for p in (q, q + 1)
                ]
                outs.append(applied(layer, blocks))
            values = []
            for tile in range(8):
                value = jnp.concatenate(
                    [outs[q // 2][16 * tile : 16 * tile + 16, GATE * (q % 2) : GATE * (q % 2 + 1)] for q in range(8)], 0
                )
                values.append(turned_sum(picks_ref[1 + layer // 4], value))
            for tile in range(8):
                target[tile * GATE : (tile + 1) * GATE, :] = values[tile]
        else:
            blocks = [two_parts(rows(source, layer, i * 16, 16)) for i in range(8)]
            out = applied(layer, blocks)
            for i in range(8):
                target[i * GATE : (i + 1) * GATE, :] = out[:, GATE * i : GATE * (i + 1)]
        source, target = target, source
    last = jnp.concatenate([picks_ref[3]] * 2, 0)
    values = [rows(source, LAYERS, tile * 16, 16) for tile in range(8)]
    values = [dot(jnp.concatenate(two_parts(value.T), 1), last) for value in values]
    for tile in range(8):
        ends[:, tile, :] = values[tile][:64]
        ends[:, 8 + tile, :] = values[tile][64:]
    core = core_ref[0]
    for pair in range(32):
        out_ref[pair, core] = ends[2 * pair + core]
        send_ref[pair] = ends[2 * pair + 1 - core]


def evolve(core, state, gates, moves, perms):
    return pl.pallas_call(
        evolve_kernel,
        out_shape=(
            jax.ShapeDtypeStruct((32, 2, 16, GATE), F32),
            jax.ShapeDtypeStruct((32, 16, GATE), F32),
        ),
        in_specs=[pl.BlockSpec(memory_space=pltpu.SMEM)] + [pl.BlockSpec(memory_space=pltpu.VMEM)] * 4,
        out_specs=(pl.BlockSpec(memory_space=pltpu.VMEM),) * 2,
        scratch_shapes=[
            pltpu.VMEM((WIDE, GATE), F32),
            pltpu.VMEM((WIDE, GATE), F32),
            pltpu.VMEM((64, 16, GATE), F32),
        ],
        compiler_params=pltpu.CompilerParams(vmem_limit_bytes=24 * 2**20),
        cost_estimate=pl.CostEstimate(flops=6 * 10**9, bytes_accessed=20 * 2**20, transcendentals=0),
        name="evolve",
    )(core, state, gates, moves, perms)


def body(amplitudes, gate_stack, targets):
    core = lax.axis_index("core").astype(I32)
    state = amplitudes.reshape(64, 16, 128)
    state = lax.all_to_all(state, ("z", "yx", "core"), split_axis=0, concat_axis=0, tiled=True)
    kept, sent = evolve(core[None], state, *prepare(targets, gate_stack))
    got = lax.ppermute(sent, "core", [(0, 1), (1, 0)])
    state = lax.dynamic_update_slice_in_dim(kept, got[:, None], 1 - core, 1)
    state = lax.all_to_all(state, ("z", "yx"), split_axis=0, concat_axis=0, tiled=True)
    return state.reshape(amplitudes.shape)


def solution(mesh):
    split = Mesh(mesh.devices.reshape(2, 4, 8, 2), ("top", "z", "yx", "core"))
    place = P(("top", "z"), ("yx", "core"), None)
    return jax.shard_map(body, mesh=split, in_specs=(place, P(), P()), out_specs=place, check_vma=False)
```
